256 devices in a mesh: gx: 64 (over y, x, z_hi), gy: 4 (over z_lo, core).
Axes of the slice: x: 4, y: 4, z: 8 (z_hi: 4, z_lo: 2; z = z_hi * 2 + z_lo), core: 2. Of those that a mesh axis runs over, the one named last changes fastest.
Arguments:
- query_feats: bfloat16 [64, 4, 512, 768], P('gx', 'gy'), may hold values from -16 to 16
- anchors: bfloat16 [128, 8, 128, 768], P('gx', 'gy'), may hold values from -16 to 16
- tile_lists: int32 [64, 4, 4, 4], P('gx', 'gy'), may hold values from 0 to 15, as said below
- tile_counts: int32 [64, 4, 4], P('gx', 'gy'), may hold values from 1 to 4, as said below
- out_grad: bfloat16 [64, 4, 512, 768], P('gx', 'gy'), may hold values from -6 to 6
- w_query: bfloat16 [768, 768], replicated, may hold values from -0.21875 to 0.21875
- w_key: bfloat16 [768, 768], replicated, may hold values from -0.21875 to 0.21875
- w_value: bfloat16 [768, 768], replicated, may hold values from -0.21875 to 0.21875
- w_out: bfloat16 [768, 768], replicated, may hold values from -0.21875 to 0.21875
Outputs:
- query_grad: bfloat16 [64, 4, 512, 768], P('gx', 'gy')
- anchor_grad: bfloat16 [128, 8, 128, 768], P('gx', 'gy')
- weight_grads: float32 [3072, 768], P(('gx', 'gy'))
The draws below stay inside these ranges and needn't reach their ends.
Inputs may be any that keep to these rules, and one draw needn't show every extreme that they name: `tile_lists`: within one block the 4 entries are distinct, and each names a window tile that lies inside the grid. `tile_counts`: every brick has a level; its first block's count equals the level and no count of the brick exceeds it. Some brick's level is 4.
All inputs are finite; a program needn't handle non-finite values.
Results may differ from the reference program's by a relative error of at most 0.029.
The reference program's roundings to bfloat16 on the way count: a program that leaves them out, or rounds other values in their place, can miss the bound.
Values may be sent and summed in bfloat16 or wider, within the bound.
A program may use at most 192 MiB of HBM per device.

```python
import jax
import jax.numpy as jnp
from jax import lax

D = 768
HEADS = 12
HEAD_DIM = 64
TILE = 128
KT = 4
AX = 2
AY = 2
Q_DEV = 512
GRID_X = 64
GRID_Y = 4
TX = 128
TY = 8
WIN = 16
QBLK = 4
TOKENS = 131072


def draw_query_feats(key, part):
    key = jax.random.fold_in(key, 11)
    key_base = jax.random.fold_in(key, 0)
    shape = (GRID_X, GRID_Y, Q_DEV, D)
    return jnp.clip(jax.random.normal(key_base, shape, jnp.float32), -6.0, 6.0).astype(jnp.bfloat16)


def draw_anchors(key, part):
    key = jax.random.fold_in(key, 13)
    shape = (TX, TY, TILE, D)
    return jnp.clip(jax.random.normal(key, shape, jnp.float32), -6.0, 6.0).astype(jnp.bfloat16)


def draw_tile_lists(key, part):
    key = jax.random.fold_in(key, 5)
    across = AY + 2
    tiles = (AX + 2) * across
    slot = jnp.arange(tiles, dtype=jnp.int32)
    place_x = jnp.arange(GRID_X, dtype=jnp.int32)[:, None, None] * AX + slot[None, None, :] // across - 1
    place_y = jnp.arange(GRID_Y, dtype=jnp.int32)[None, :, None] * AY + slot[None, None, :] % across - 1
    inside = (place_x >= 0) & (place_x < TX) & (place_y >= 0) & (place_y < TY)
    noise = jax.random.randint(key, (GRID_X, GRID_Y, QBLK, tiles), 0, 1 << 20)
    ranked = noise + jnp.where(inside, 0, 1 << 21)[:, :, None, :]
    order = jnp.argsort(ranked, axis=-1, stable=True)
    return order[..., :KT].astype(jnp.int32)


def draw_tile_counts(key, part):
    key = jax.random.fold_in(key, 9)
    key_level, key_each = jax.random.split(key)
    level = jax.random.randint(key_level, (GRID_X, GRID_Y, 1), 1, KT + 1)
    level = level.at[0, 0, 0].set(KT)
    each = 1 + jax.random.randint(key_each, (GRID_X, GRID_Y, QBLK), 0, 1 << 20) % level
    each = each.at[:, :, 0].set(level[:, :, 0])
    return each.astype(jnp.int32)


def levels(key, shape, shards, least, high):
    factor_of = 1.0
    for axis_at, shards_of in shards:
        steps = jax.random.uniform(jax.random.fold_in(jax.random.fold_in(key, 6), axis_at), (shards_of,), jnp.float32, least / len(shards), high / len(shards))
        factor_of = factor_of * jnp.repeat(jnp.exp(steps), shape[axis_at] // shards_of).reshape((-1,) + (1,) * (len(shape) - 1 - axis_at))
    return factor_of


def bell_draw(key, dims, width, reach, cuts=(), held_as=jnp.bfloat16):
    drawn = jax.random.normal(key, dims, jnp.float32) * width
    if len(cuts) > 0:
        drawn = levels(key, dims, cuts, -0.22, 0.18) * drawn
    return jnp.clip(drawn, min=-reach, max=reach).astype(held_as)


def setup_inputs(seed: int = 0) -> dict:
    key_list = jax.random.split(jax.random.key(seed), 10)
    query_feats = draw_query_feats(jax.random.fold_in(key_list[9], 71), 0)
    anchors = draw_anchors(jax.random.fold_in(key_list[9], 71), 0)
    tile_lists = draw_tile_lists(jax.random.fold_in(key_list[9], 71), 0)
    tile_counts = draw_tile_counts(jax.random.fold_in(key_list[9], 71), 0)
    out_grad = bell_draw(key_list[4], (GRID_X, GRID_Y, Q_DEV, D), 1.0, 6.0, ((0, 64), (1, 4)))
    w_query = bell_draw(key_list[5], (D, D), D ** -0.5, 0.21875)
    w_key = bell_draw(key_list[6], (D, D), D ** -0.5, 0.21875)
    w_value = bell_draw(key_list[7], (D, D), D ** -0.5, 0.21875)
    w_out = bell_draw(key_list[8], (D, D), D ** -0.5, 0.21875)
    return dict(query_feats=query_feats, anchors=anchors, tile_lists=tile_lists, tile_counts=tile_counts, out_grad=out_grad, w_query=w_query, w_key=w_key, w_value=w_value, w_out=w_out)


def local_grads(query_proj, dout_proj, lists, counts, window):
    blocks = lists.shape[0]
    key_count = KT * TILE
    picked = window[lists.reshape(-1)].reshape(blocks, key_count, 2 * D)
    key_blk = picked[:, :, :D].reshape(blocks, key_count, HEADS, HEAD_DIM).astype(jnp.float32)
    value_blk = picked[:, :, D:].reshape(blocks, key_count, HEADS, HEAD_DIM).astype(jnp.float32)
    query_blk = query_proj.reshape(blocks, TILE, HEADS, HEAD_DIM).astype(jnp.float32)
    dout_blk = dout_proj.reshape(blocks, TILE, HEADS, HEAD_DIM).astype(jnp.float32)
    scale = HEAD_DIM ** -0.5
    scores = jnp.einsum("bqhd,bkhd->bhqk", query_blk, key_blk) * scale
    slot_of = jnp.arange(key_count, dtype=jnp.int32)[None, :] // TILE
    live = slot_of < counts[:, None]
    scores = jnp.where(live[:, None, None, :], scores, -jnp.inf)
    row_max = jnp.max(scores, axis=-1, keepdims=True)
    expo_vals = jnp.exp(scores - row_max)
    prob_full = expo_vals / jnp.sum(expo_vals, axis=-1, keepdims=True)
    prob_half = prob_full.astype(jnp.bfloat16).astype(jnp.float32)
    attended = jnp.einsum("bhqk,bkhd->bqhd", prob_half, value_blk).astype(jnp.bfloat16)
    dprob = jnp.einsum("bqhd,bkhd->bhqk", dout_blk, value_blk)
    row_delta = jnp.einsum("bqhd,bqhd->bhq", dout_blk, attended.astype(jnp.float32))
    dscore = (prob_full * (dprob - row_delta[..., None])).astype(jnp.bfloat16).astype(jnp.float32)
    dquery = (jnp.einsum("bhqk,bkhd->bqhd", dscore, key_blk) * scale).astype(jnp.bfloat16)
    dkey = jnp.einsum("bhqk,bqhd->bkhd", dscore, query_blk) * scale
    dvalue = jnp.einsum("bhqk,bqhd->bkhd", prob_half, dout_blk)
    slot_grads = jnp.concatenate(
        [dkey.reshape(blocks * KT, TILE, D), dvalue.reshape(blocks * KT, TILE, D)], axis=-1)
    window_grads = jnp.zeros((window.shape[0], TILE, 2 * D), jnp.float32).at[lists.reshape(-1)].add(slot_grads)
    return window_grads, dquery.reshape(blocks * TILE, D), attended.reshape(blocks * TILE, D)


def reference(query_feats, anchors, tile_lists, tile_counts, out_grad, w_query, w_key, w_value, w_out):
    w_pair = jnp.concatenate([w_key, w_value], axis=1)
    flat_anchor = anchors.reshape(-1, D)
    pairs = jnp.dot(flat_anchor, w_pair, preferred_element_type=jnp.float32).astype(jnp.bfloat16)
    pairs = pairs.reshape(TX, TY, TILE, 2 * D)
    padded = jnp.pad(pairs, ((1, 1), (1, 1), (0, 0), (0, 0)))
    devices = GRID_X * GRID_Y
    query_rows = query_feats.reshape(devices, Q_DEV, D)
    dout_rows = out_grad.reshape(devices, Q_DEV, D)
    list_rows = tile_lists.reshape(devices, QBLK, KT)
    count_rows = tile_counts.reshape(devices, QBLK)
    zero = jnp.zeros((), jnp.int32)
    shape = (AX + 2, AY + 2, TILE, 2 * D)

    def device_step(carry, index):
        grad_pad, grad_query_w, grad_out_w = carry
        row_x = (index // GRID_Y).astype(jnp.int32)
        row_y = (index % GRID_Y).astype(jnp.int32)
        corner = (row_x * AX, row_y * AY, zero, zero)
        window = lax.dynamic_slice(padded, corner, shape).reshape(WIN, TILE, 2 * D)
        queries_in = query_rows[index]
        dout_in = dout_rows[index]
        query_proj = jnp.dot(queries_in, w_query, preferred_element_type=jnp.float32).astype(jnp.bfloat16)
        dout_proj = jnp.dot(dout_in, w_out.T, preferred_element_type=jnp.float32).astype(jnp.bfloat16)
        window_grads, dquery, attended = local_grads(query_proj, dout_proj, list_rows[index], count_rows[index], window)
        partial_half = lax.optimization_barrier(window_grads.astype(jnp.bfloat16))
        partial_back = partial_half.astype(jnp.float32).reshape(shape)
        grad_pad = lax.dynamic_update_slice(grad_pad, lax.dynamic_slice(grad_pad, corner, shape) + partial_back, corner)
        grad_query_w = grad_query_w + jnp.dot(queries_in.T, dquery, preferred_element_type=jnp.float32)
        grad_out_w = grad_out_w + jnp.dot(attended.T, dout_in, preferred_element_type=jnp.float32)
        query_grad = jnp.dot(dquery, w_query.T, preferred_element_type=jnp.float32).astype(jnp.bfloat16)
        return (grad_pad, grad_query_w, grad_out_w), query_grad

    start = (jnp.zeros((TX + 2, TY + 2, TILE, 2 * D), jnp.float32),
             jnp.zeros((D, D), jnp.float32), jnp.zeros((D, D), jnp.float32))
    (grad_pad, grad_query_w, grad_out_w), query_grad = lax.scan(
        device_step, start, jnp.arange(devices, dtype=jnp.int32))
    pair_grads = grad_pad[1:-1, 1:-1].astype(jnp.bfloat16).reshape(-1, 2 * D)
    anchor_grad = jnp.dot(pair_grads, w_pair.T, preferred_element_type=jnp.float32).astype(jnp.bfloat16)
    grad_pair_w = jnp.dot(flat_anchor.T, pair_grads, preferred_element_type=jnp.float32)
    weight_grads = jnp.concatenate(
        [grad_query_w, grad_pair_w[:, :D], grad_pair_w[:, D:], grad_out_w], axis=0) * (TOKENS ** -0.5)
    return (query_grad.reshape(GRID_X, GRID_Y, Q_DEV, D),
            anchor_grad.reshape(TX, TY, TILE, D), weight_grads)
```

```python
from functools import partial

import jax
import jax.numpy as jnp
from jax import lax
from jax.experimental import pallas as pl
from jax.experimental.pallas import tpu as pltpu
from jax.sharding import PartitionSpec as P

HEADS = 12
HEAD_DIM = 64
KT = 4
D = 768
TILE = 128
PAIRS = 6
Q_DEV = 512
SCALE = HEAD_DIM ** (-0.5)
HALF = 384
NEG = -1e30
MESH = pl.DeviceIdType.MESH
F32 = jnp.float32
BF16 = jnp.bfloat16
VMEM_BYTES = 56 * 1024 * 1024

DIRS = ((-1, 0), (1, 0), (-1, -1), (-1, 1), (1, -1), (1, 1), (0, -1), (0, 1))
OWN = {-1: (0, 1), 0: (0, 2), 1: (1, 2)}
LAND = {-1: (3, 4), 0: (1, 3), 1: (0, 1)}
ROWS = {-1: (1,), 0: (0, 1), 1: (0,)}


def nn(left, right):
    return lax.dot_general(left, right, (((1,), (0,)), ((), ())), preferred_element_type=F32)


def nt(left, right):
    return lax.dot_general(left, right, (((1,), (1,)), ((), ())), preferred_element_type=F32)


def tn(left, right):
    return lax.dot_general(left, right, (((0,), (0,)), ((), ())), preferred_element_type=F32)


def inside(place, extents):
    (px, py), (nx, ny) = place, extents
    return (px >= 0) & (px < nx) & (py >= 0) & (py < ny)


def greet(partners):
    barrier = pltpu.get_barrier_semaphore()
    total = jnp.int32(0)
    for where, present in partners:
        @pl.when(present)
        def _():
            pl.semaphore_signal(barrier, inc=1, device_id=where, device_id_type=MESH)
        total = total + jnp.where(present, 1, 0).astype(jnp.int32)
    pl.semaphore_wait(barrier, total)


def halo_kernel(
    extents,
    anchors, qf_in, do_in, wq_in, wk_in, wv_in, wo_in,
    kw_out, vw_out, awt_out, q_out, dp_out, dpt_out, qft_out,
    win, kw, vw, awt, qf, do, wq, wk, wv, wo, q_s, dp_s, dpt_s, qft_s,
    send_sem, recv_sem, load_sem, store_sem,
):
    gx, gy = lax.axis_index("gx"), lax.axis_index("gy")
    loads = [
        pltpu.make_async_copy(src, dst, load_sem.at[i])
        for i, (src, dst) in enumerate(
            [(qf_in, qf), (wq_in, wq), (do_in, do), (wo_in, wo), (wk_in, wk), (wv_in, wv)]
        )
    ]
    own = pltpu.make_async_copy(anchors, win.at[1:3, 1:3], load_sem.at[6])
    for load in loads:
        load.start()
    own.start()
    greet([((gx + dx, gy + dy), inside((gx + dx, gy + dy), extents)) for dx, dy in DIRS])

    def sending(i):
        dx, dy = DIRS[i]
        (r0, r1), (c0, c1) = OWN[dx], OWN[dy]
        (p0, p1), (q0, q1) = LAND[dx], LAND[dy]
        return pltpu.make_async_remote_copy(
            src_ref=anchors.at[r0:r1, c0:c1],
            dst_ref=win.at[p0:p1, q0:q1],
            send_sem=send_sem.at[i],
            recv_sem=recv_sem.at[i],
            device_id=(gx + dx, gy + dy),
            device_id_type=MESH,
        )

    for i, (dx, dy) in enumerate(DIRS):
        @pl.when(inside((gx + dx, gy + dy), extents))
        def _(i=i):
            sending(i).start()

    for dx, dy in DIRS:
        (p0, p1), (q0, q1) = LAND[dx], LAND[dy]

        @pl.when(jnp.logical_not(inside((gx - dx, gy - dy), extents)))
        def _(p0=p0, p1=p1, q0=q0, q1=q1):
            win[p0:p1, q0:q1] = jnp.zeros((p1 - p0, q1 - q0, TILE, D), BF16)

    loads[0].wait()
    loads[1].wait()

    def project_query(j, _):
        at = pl.ds(pl.multiple_of(j * 256, 256), 256)
        q_s[:, at] = (nn(qf[...], wq[:, at]).astype(BF16) * SCALE).astype(BF16)
        return 0

    lax.fori_loop(0, 3, project_query, 0)
    loads[2].wait()
    loads[3].wait()

    def project_dout(j, _):
        at = pl.ds(pl.multiple_of(j * 256, 256), 256)
        dp_s[:, at] = nt(do[...], wo[at, :]).astype(BF16)
        dpt_s[at, :] = nt(wo[at, :], do[...]).astype(BF16)
        qft_s[at, :] = qf[:, at].T
        return 0

    lax.fori_loop(0, 3, project_dout, 0)
    stores = []

    def store(src, dst):
        copy = pltpu.make_async_copy(src, dst, store_sem.at[len(stores)])
        copy.start()
        stores.append(copy)

    store(q_s, q_out)
    store(dp_s, dp_out)
    store(dpt_s, dpt_out)
    store(qft_s, qft_out)
    loads[4].wait()
    loads[5].wait()
    own.wait()

    def project_tiles(places):
        rows = jnp.concatenate([win[r, c] for r, c in places], axis=0)

        def step(j, _):
            at = pl.ds(pl.multiple_of(j * 256, 256), 256)
            for weight, goal in ((wk, kw), (wv, vw)):
                part = nn(rows, weight[:, at]).astype(BF16)
                for n, (r, c) in enumerate(places):
                    for i in range(2):
                        goal[2 * j + i, r * 4 + c] = part[
                            n * TILE : (n + 1) * TILE, i * TILE : (i + 1) * TILE
                        ]
            return 0

        lax.fori_loop(0, 3, step, 0)
        for r, c in places:
            awt[r * 4 + c] = win[r, c].T

    def arrive(dx, dy):
        @pl.when(inside((gx - dx, gy - dy), extents))
        def _():
            sending(DIRS.index((dx, dy))).wait_recv()

    project_tiles([(1, 1), (1, 2), (2, 1), (2, 2)])
    arrive(0, 1)
    project_tiles([(1, 0), (2, 0)])
    arrive(0, -1)
    project_tiles([(1, 3), (2, 3)])
    store(kw.at[:, 4:12], kw_out.at[:, 4:12])
    store(vw.at[:, 4:12], vw_out.at[:, 4:12])
    store(awt.at[4:12], awt_out.at[4:12])
    for dx, first in ((1, 0), (-1, 12)):
        for dy in (0, -1, 1):
            arrive(dx, dy)
        project_tiles([(first // 4, c) for c in range(4)])
        store(kw.at[:, first : first + 4], kw_out.at[:, first : first + 4])
        store(vw.at[:, first : first + 4], vw_out.at[:, first : first + 4])
        store(awt.at[first : first + 4], awt_out.at[first : first + 4])
    for i, (dx, dy) in enumerate(DIRS):
        @pl.when(inside((gx + dx, gy + dy), extents))
        def _(i=i):
            sending(i).wait_send()
    for copy in stores:
        copy.wait()


def halo(extents, anchors, qf, do, wq, wk, wv, wo):
    any_spec = pl.BlockSpec(memory_space=pl.ANY)
    blocks = (PAIRS, 16, TILE, TILE)
    tall, wide = (Q_DEV, D), (D, Q_DEV)
    square = (D, D)
    shapes = [blocks, blocks, (16, D, TILE), tall, tall, wide, wide]
    return pl.pallas_call(
        partial(halo_kernel, extents),
        name="halo",
        out_shape=[jax.ShapeDtypeStruct(s, BF16) for s in shapes],
        in_specs=[any_spec] * 7,
        out_specs=[any_spec] * 7,
        scratch_shapes=[
            pltpu.VMEM(s, BF16)
            for s in [(4, 4, TILE, D), blocks, blocks, (16, D, TILE), tall, tall,
                      square, square, square, square, tall, tall, wide, wide]
        ]
        + [
            pltpu.SemaphoreType.DMA((8,)),
            pltpu.SemaphoreType.DMA((8,)),
            pltpu.SemaphoreType.DMA((7,)),
            pltpu.SemaphoreType.DMA((13,)),
        ],
        compiler_params=pltpu.CompilerParams(
            collective_id=0, has_side_effects=True, vmem_limit_bytes=VMEM_BYTES
        ),
    )(anchors, qf, do, wq, wk, wv, wo)


def attention_kernel(
    lists, counts, kw, vw, q_ref, dp_ref, dpt_ref,
    pk_out, pv_out, att_out, dq_out, dk, dv,
):
    dk[...] = jnp.zeros_like(dk)
    dv[...] = jnp.zeros_like(dv)
    lane = lax.broadcasted_iota(jnp.int32, (TILE, TILE), 1)
    first = lane < HEAD_DIM
    for b in range(4):
        tiles = [lists[b * KT + s] for s in range(KT)]
        count = counts[b]
        at = slice(b * TILE, (b + 1) * TILE)
        q = q_ref[at, :]
        do = dp_ref[at, :]
        zero = jnp.zeros_like(q)
        q2 = jnp.concatenate([jnp.where(first, q, zero), jnp.where(first, zero, q)], axis=0)
        do2 = jnp.concatenate([jnp.where(first, do, zero), jnp.where(first, zero, do)], axis=0)
        keys = jnp.concatenate([kw[0, t] for t in tiles], axis=0)
        values = jnp.concatenate([vw[0, t] for t in tiles], axis=0)
        scores = nt(keys, q2)
        scores = jnp.concatenate(
            [
                scores[s * TILE : (s + 1) * TILE] + jnp.where(s < count, 0.0, NEG).astype(F32)
                for s in range(KT)
            ],
            axis=0,
        )
        top = jnp.max(scores, axis=0, keepdims=True)
        expo = jnp.exp(scores - top)
        prob = expo * (1.0 / jnp.sum(expo, axis=0, keepdims=True))
        half = prob.astype(BF16)
        att2 = tn(values, half)
        att = jnp.concatenate(
            [att2[:HEAD_DIM, :TILE], att2[HEAD_DIM:, TILE:]], axis=0
        ).astype(BF16)
        att_out[:, at] = att
        both = att.astype(F32) * dpt_ref[:, at].astype(F32)
        delta = jnp.concatenate(
            [
                jnp.sum(both[:HEAD_DIM], axis=0, keepdims=True),
                jnp.sum(both[HEAD_DIM:], axis=0, keepdims=True),
            ],
            axis=1,
        )
        dprob = nt(values, do2)
        dscore = (prob * (dprob - delta)).astype(BF16)
        dq2 = tn(keys, dscore)
        dq = jnp.concatenate([dq2[:HEAD_DIM, :TILE], dq2[HEAD_DIM:, TILE:]], axis=0) * SCALE
        dq_out[at, :] = dq.T.astype(BF16)
        dkey = nn(dscore, q2)
        dvalue = nn(half, do2)
        for s in range(KT):
            dk[tiles[s]] += dkey[s * TILE : (s + 1) * TILE]
            dv[tiles[s]] += dvalue[s * TILE : (s + 1) * TILE]
    pk_out[0] = dk[...].astype(BF16)
    pv_out[0] = dv[...].astype(BF16)


def attention(lists, counts, kw, vw, q, dp, dpt):
    blocks = (PAIRS, 16, TILE, TILE)
    by_pair = pl.BlockSpec((1, 16, TILE, TILE), lambda h, *_: (h, 0, 0, 0))
    tall = pl.BlockSpec((Q_DEV, TILE), lambda h, *_: (0, h))
    wide = pl.BlockSpec((TILE, Q_DEV), lambda h, *_: (h, 0))
    return pl.pallas_call(
        attention_kernel,
        name="attention",
        out_shape=[
            jax.ShapeDtypeStruct(blocks, BF16),
            jax.ShapeDtypeStruct(blocks, BF16),
            jax.ShapeDtypeStruct((D, Q_DEV), BF16),
            jax.ShapeDtypeStruct((Q_DEV, D), BF16),
        ],
        grid_spec=pltpu.PrefetchScalarGridSpec(
            num_scalar_prefetch=2,
            grid=(PAIRS,),
            in_specs=[by_pair, by_pair, tall, tall, wide],
            out_specs=[by_pair, by_pair, wide, tall],
            scratch_shapes=[pltpu.VMEM((16, TILE, TILE), F32), pltpu.VMEM((16, TILE, TILE), F32)],
        ),
        compiler_params=pltpu.CompilerParams(vmem_limit_bytes=VMEM_BYTES),
    )(lists, counts, kw, vw, q, dp, dpt)


def grads_kernel(
    extents,
    pk_in, pv_in, awt_in, qft_in, att_in, dq_in, do_in, wq_in, wk_in, wv_in,
    ag_out, qg_out, wg_out,
    pk, pv, awt, qft, att, dq, do, wq, wk, wv,
    snd, rcv, acc, qg_s, ag_s, wg_s,
    mine, core_s, core_r, term, ya_r, xb_r, ta, tb, xa_r, yb_r, zs, zr, fs, fr,
    load_sem, store_sem, hs_sem, hr_sem, cs_sem, cr_sem,
    yas_sem, yar_sem, xbs_sem, xbr_sem, xas_sem, xar_sem, ybs_sem, ybr_sem,
    zs_sem, zr_sem, f_sem,
):
    gx, gy = lax.axis_index("gx"), lax.axis_index("gy")
    core = lax.rem(gy, 2)
    z = lax.rem(gx, 4) * 2 + gy // 2
    x = lax.rem(gx // 4, 4)
    y = gx // 16

    def device(y, x, z, core):
        return ((y * 4 + x) * 4 + z // 2, lax.rem(z, 2) * 2 + core)

    pairs = [(pk_in, pk), (pv_in, pv), (wk_in, wk), (wv_in, wv), (qft_in, qft), (dq_in, dq),
             (att_in, att), (do_in, do), (awt_in, awt), (wq_in, wq)]
    loads = [pltpu.make_async_copy(s, d, load_sem.at[i]) for i, (s, d) in enumerate(pairs)]
    for load in loads:
        load.start()
    sibling = device(y, x, z, 1 - core)
    around = [((gx + dx, gy + dy), inside((gx + dx, gy + dy), extents)) for dx, dy in DIRS]
    always = gx >= 0
    fixed = [sibling]
    fixed += [device(lax.rem(y + k, 4), x, z, core) for k in (1, 2, 3)]
    fixed += [device(y, lax.rem(x + k, 4), z, core) for k in (1, 2, 3)]
    fixed += [device(y, x, lax.rem(z + k, 8), core) for k in range(1, 8)]
    greet(around + [(where, always) for where in fixed])

    def remote(src, dst, send, recv, where):
        return pltpu.make_async_remote_copy(
            src_ref=src, dst_ref=dst, send_sem=send, recv_sem=recv,
            device_id=where, device_id_type=MESH,
        )

    def returning(i):
        dx, dy = DIRS[i]
        row, col = {-1: 0, 1: 3}.get(dx), {-1: 0, 1: 3}.get(dy)
        if row is None:
            src, dst = snd.at[1:3, col], rcv.at[i]
        elif col is None:
            src, dst = snd.at[row, 1:3], rcv.at[i]
        else:
            src, dst = snd.at[row, col], rcv.at[i, 0]
        return remote(src, dst, hs_sem.at[i], hr_sem.at[i], (gx + dx, gy + dy))

    def terms_of(places, keep):
        def side(blocks):
            return jnp.concatenate(
                [
                    jnp.concatenate([blocks[h, r * 4 + c] for r, c in places], axis=0)
                    for h in range(PAIRS)
                ],
                axis=1,
            )

        left_k, left_v = side(pk), side(pv)

        def step(j, _):
            at = pl.ds(pl.multiple_of(j * 256, 256), 256)
            part = nt(left_k, wk[at, :]) + nt(left_v, wv[at, :])
            for n, (r, c) in enumerate(places):
                piece = part[n * TILE : (n + 1) * TILE]
                if keep:
                    acc[r - 1, c - 1, :, at] = piece
                else:
                    snd[r, c, :, at] = piece.astype(BF16)
            return 0

        lax.fori_loop(0, 3, step, 0)

    def send_back(dirs):
        for dx, dy in dirs:
            @pl.when(inside((gx + dx, gy + dy), extents))
            def _(dx=dx, dy=dy):
                returning(DIRS.index((dx, dy))).start()

    for i in range(4):
        loads[i].wait()
    terms_of([(0, c) for c in range(4)], False)
    send_back([(-1, 0), (-1, -1), (-1, 1)])
    terms_of([(3, c) for c in range(4)], False)
    send_back([(1, 0), (1, -1), (1, 1)])
    terms_of([(1, 0), (2, 0), (1, 3), (2, 3)], False)
    send_back([(0, -1), (0, 1)])

    def weight_halves(m, rows_of, columns_of):
        def step(n, _):
            half = jnp.where(n == 0, 1 - core, core)
            part = nn(rows_of(), columns_of(half))

            @pl.when(n == 0)
            def _():
                core_s[m] = part.astype(BF16)

            @pl.when(n == 1)
            def _():
                mine[m] = part
            return 0

        lax.fori_loop(0, 2, step, 0)
        crossing(m).start()

    def crossing(m):
        return remote(core_s.at[m], core_r.at[m], cs_sem.at[m], cr_sem.at[m], sibling)

    def to_row(m):
        k = lax.rem(m - y + 4, 4)
        slot = lax.rem(3 - k + 4, 4)
        return remote(term.at[m, :, 0], ya_r.at[slot], yas_sem.at[m], yar_sem.at[slot],
                      device(m, x, z, core))

    def to_column(m, k):
        goal = lax.rem(x + k, 4)
        return remote(term.at[m, goal, 1], xb_r.at[3 - k, m], xbs_sem.at[k - 1, m],
                      xbr_sem.at[3 - k, m], device(y, goal, z, core))

    def add_cores(m):
        crossing(m).wait()
        for goal in range(4):
            for part in range(2):
                at = slice(goal * 192 + part * 96, goal * 192 + part * 96 + 96)
                term[m, goal, part] = (mine[m, at] + core_r[m, at].astype(F32)).astype(BF16)

        @pl.when(y != m)
        def _():
            to_row(m).start()

        for k in (2, 1, 3):
            to_column(m, k).start()

    def lanes(ref, half):
        return ref[:, pl.ds(pl.multiple_of(half * HALF, 128), HALF)]

    def stacked(ref, half):
        return jnp.concatenate(
            [ref[half * 3 + i].reshape(16 * TILE, TILE) for i in range(3)], axis=1
        )

    def anchor_rows():
        return jnp.concatenate([awt[t] for t in range(16)], axis=1)

    for i in range(4, 8):
        loads[i].wait()
    weight_halves(0, lambda: qft[...], lambda half: lanes(dq, half))
    weight_halves(3, lambda: att[...], lambda half: lanes(do, half))
    add_cores(0)
    add_cores(3)
    loads[8].wait()
    weight_halves(1, anchor_rows, lambda half: stacked(pk, half))
    weight_halves(2, anchor_rows, lambda half: stacked(pv, half))
    add_cores(1)
    add_cores(2)

    terms_of([(1, 1), (1, 2), (2, 1), (2, 2)], True)
    loads[9].wait()

    def query_grad(j, _):
        at = pl.ds(pl.multiple_of(j * 256, 256), 256)
        qg_s[:, at] = nt(dq[...], wq[at, :]).astype(BF16)
        return 0

    lax.fori_loop(0, 3, query_grad, 0)
    qg_copy = pltpu.make_async_copy(qg_s, qg_out, store_sem.at[0])
    qg_copy.start()

    for slot in range(3):
        remote(term.at[0, :, 0], ya_r.at[slot], yas_sem.at[0], yar_sem.at[slot],
               sibling).wait_recv()
    for goal in range(4):
        total = term[y, goal, 0].astype(F32)
        for slot in range(3):
            total = total + ya_r[slot, goal].astype(F32)
        ta[goal] = total.astype(BF16)

    def to_column_second(k):
        goal = lax.rem(x + k, 4)
        return remote(ta.at[goal], xa_r.at[3 - k], xas_sem.at[k - 1], xar_sem.at[3 - k],
                      device(y, goal, z, core))

    for k in (2, 1, 3):
        to_column_second(k).start()
    for k in (1, 2, 3):
        for m in range(4):
            to_column(m, k).wait_recv()
    for m in range(4):
        total = term[m, x, 1].astype(F32)
        for slot in range(3):
            total = total + xb_r[slot, m].astype(F32)
        tb[m] = total.astype(BF16)

    def to_row_second(k):
        goal = lax.rem(y + k, 4)
        return remote(tb.at[goal], yb_r.at[3 - k], ybs_sem.at[k - 1], ybr_sem.at[3 - k],
                      device(goal, x, z, core))

    for k in (2, 1, 3):
        to_row_second(k).start()

    zs[:, 16:32] = jnp.zeros((8, 16, HALF), BF16)
    for k in (1, 2, 3):
        to_column_second(k).wait_recv()
    total = ta[x].astype(F32)
    for slot in range(3):
        total = total + xa_r[slot].astype(F32)
    for i in range(4):
        zs[i, 0:24] = total[i * 24 : (i + 1) * 24].astype(BF16)
    for k in (1, 2, 3):
        to_row_second(k).wait_recv()
    total = tb[y].astype(F32)
    for slot in range(3):
        total = total + yb_r[slot].astype(F32)
    for i in range(4):
        zs[4 + i, 0:24] = total[i * 24 : (i + 1) * 24].astype(BF16)

    def along(k):
        goal = lax.rem(z + k, 8)
        return remote(zs.at[goal], zr.at[7 - k], zs_sem.at[k - 1], zr_sem.at[7 - k],
                      device(y, x, goal, core))

    for k in (4, 3, 5, 2, 6, 1, 7):
        along(k).start()

    for dx, dy in ((0, -1), (0, 1), (-1, 0), (1, 0), (-1, -1), (-1, 1), (1, -1), (1, 1)):
        i = DIRS.index((dx, dy))

        @pl.when(inside((gx - dx, gy - dy), extents))
        def _(i=i, dx=dx, dy=dy):
            returning(i).wait_recv()
            n = 0
            for r in ROWS[dx]:
                for c in ROWS[dy]:
                    acc[r, c] += rcv[i, n].astype(F32)
                    n += 1

    ag_s[...] = acc[...].astype(BF16)
    ag_copy = pltpu.make_async_copy(ag_s, ag_out, store_sem.at[1])
    ag_copy.start()

    for k in range(1, 8):
        along(k).wait_recv()
    total = zs[z].astype(F32)
    for slot in range(7):
        total = total + zr[slot].astype(F32)
    fs[...] = total[0:24]
    last = remote(fs, fr, f_sem.at[0], f_sem.at[1], sibling)
    last.start()
    last.wait()
    low = core == 0
    held, other = fs[...], fr[...]
    held = jnp.where(low, held[0:12], held[12:24])
    other = jnp.where(low, other[0:12], other[12:24])
    norm = (extents[0] * extents[1] * Q_DEV) ** (-0.5)
    wg_s[:, 0:HALF] = jnp.where(low, held, other) * norm
    wg_s[:, HALF:D] = jnp.where(low, other, held) * norm
    wg_copy = pltpu.make_async_copy(wg_s, wg_out, store_sem.at[2])
    wg_copy.start()

    for i, (dx, dy) in enumerate(DIRS):
        @pl.when(inside((gx + dx, gy + dy), extents))
        def _(i=i):
            returning(i).wait_send()
    for m in range(4):
        @pl.when(y != m)
        def _(m=m):
            to_row(m).wait_send()
        for k in (1, 2, 3):
            to_column(m, k).wait_send()
    for k in (1, 2, 3):
        to_column_second(k).wait_send()
        to_row_second(k).wait_send()
    for k in range(1, 8):
        along(k).wait_send()
    qg_copy.wait()
    ag_copy.wait()
    wg_copy.wait()


def grads(extents, pk, pv, awt, qft, att, dq, do, wq, wk, wv):
    any_spec = pl.BlockSpec(memory_space=pl.ANY)
    blocks = (PAIRS, 16, TILE, TILE)
    tall, wide, square = (Q_DEV, D), (D, Q_DEV), (D, D)
    dma = pltpu.SemaphoreType.DMA
    held = [
        (blocks, BF16), (blocks, BF16), ((16, D, TILE), BF16), (wide, BF16), (wide, BF16),
        (tall, BF16), (tall, BF16), (square, BF16), (square, BF16), (square, BF16),
        ((4, 4, TILE, D), BF16), ((8, 2, TILE, D), BF16), ((2, 2, TILE, D), F32), (tall, BF16),
        ((2, 2, TILE, D), BF16), ((12, D), F32),
        ((4, D, HALF), F32), ((4, D, HALF), BF16), ((4, D, HALF), BF16),
        ((4, 4, 2, 96, HALF), BF16), ((3, 4, 96, HALF), BF16), ((3, 4, 96, HALF), BF16),
        ((4, 96, HALF), BF16), ((4, 96, HALF), BF16), ((3, 96, HALF), BF16),
        ((3, 96, HALF), BF16), ((8, 32, HALF), BF16), ((7, 32, HALF), BF16),
        ((24, HALF), F32), ((24, HALF), F32),
    ]
    sems = [(10,), (3,), (8,), (8,), (4,), (4,), (4,), (3,), (3, 4), (3, 4), (3,), (3,), (3,),
            (3,), (7,), (7,), (2,)]
    return pl.pallas_call(
        partial(grads_kernel, extents),
        name="grads",
        out_shape=[
            jax.ShapeDtypeStruct((2, 2, TILE, D), BF16),
            jax.ShapeDtypeStruct(tall, BF16),
            jax.ShapeDtypeStruct((12, D), F32),
        ],
        in_specs=[any_spec] * 10,
        out_specs=[any_spec] * 3,
        scratch_shapes=[pltpu.VMEM(s, t) for s, t in held] + [dma(s) for s in sems],
        compiler_params=pltpu.CompilerParams(
            collective_id=1, has_side_effects=True, vmem_limit_bytes=VMEM_BYTES
        ),
    )(pk, pv, awt, qft, att, dq, do, wq, wk, wv)


def on_device(
    extents,
    query_feats, anchors, tile_lists, tile_counts, out_grad, w_query, w_key, w_value, w_out,
):
    qf = query_feats.reshape(Q_DEV, D)
    do = out_grad.reshape(Q_DEV, D)
    lists = tile_lists.reshape(-1)
    counts = tile_counts.reshape(-1)
    kw, vw, awt, q, dp, dpt, qft = halo(extents, anchors, qf, do, w_query, w_key, w_value, w_out)
    pk, pv, att, dq = attention(lists, counts, kw, vw, q, dp, dpt)
    anchor_grad, query_grad, weight_grads = grads(
        extents, pk, pv, awt, qft, att, dq, do, w_query, w_key, w_value
    )
    return query_grad.reshape(query_feats.shape), anchor_grad, weight_grads


def solution(mesh):
    four = P("gx", "gy", None, None)
    in_specs = (four, four, four, P("gx", "gy", None), four, P(), P(), P(), P())
    out_specs = (four, four, P(("gx", "gy"), None))
    extents = (mesh.shape["gx"], mesh.shape["gy"])
    return jax.shard_map(
        partial(on_device, extents),
        mesh=mesh, in_specs=in_specs, out_specs=out_specs, check_vma=False,
    )
```

```python
from functools import partial

import jax
import jax.numpy as jnp
from jax import lax
from jax.experimental import pallas as pl
from jax.experimental.pallas import tpu as pltpu
from jax.sharding import PartitionSpec as P

HEADS = 12
HEAD_DIM = 64
KT = 4
D = 768
TILE = 128
PAIRS = 6
Q_DEV = 512
SCALE = HEAD_DIM ** (-0.5)
HALF = 384
NEG = -1e30
MESH = pl.DeviceIdType.MESH
F32 = jnp.float32
BF16 = jnp.bfloat16
VMEM_BYTES = 56 * 1024 * 1024

DIRS = ((-1, 0), (1, 0), (-1, -1), (-1, 1), (1, -1), (1, 1), (0, -1), (0, 1))
CENTRE = ((1, 1), (1, 2), (2, 1), (2, 2))
BESIDE = ((1, 0), (2, 0), (1, 3), (2, 3))
ENDS = ((0, 1), (0, 2), (3, 1), (3, 2))
CORNERS = ((0, 0), (0, 3), (3, 0), (3, 3))
HELD = CENTRE + BESIDE + ENDS + CORNERS


def nn(left, right):
    return lax.dot_general(left, right, (((1,), (0,)), ((), ())), preferred_element_type=F32)


def nt(left, right):
    return lax.dot_general(left, right, (((1,), (1,)), ((), ())), preferred_element_type=F32)


def tn(left, right):
    return lax.dot_general(left, right, (((0,), (0,)), ((), ())), preferred_element_type=F32)


def inside(place, extents):
    (px, py), (nx, ny) = place, extents
    return (px >= 0) & (px < nx) & (py >= 0) & (py < ny)


def greet(partners):
    barrier = pltpu.get_barrier_semaphore()
    total = jnp.int32(0)
    for where, present in partners:
        @pl.when(present)
        def _():
            pl.semaphore_signal(barrier, inc=1, device_id=where, device_id_type=MESH)
        total = total + jnp.where(present, 1, 0).astype(jnp.int32)
    pl.semaphore_wait(barrier, total)


def straight(dx, dy, gy):
    return ((dx, dy) == (1, -1)) & (gy == 2) | ((dx, dy) == (-1, 1)) & (gy == 1)


def halo_kernel(
    extents,
    anchors, qf_in, do_in, wq_in, wk_in, wv_in, wo_in,
    kw_out, vw_out, awt_out, q_out, dp_out, dpt_out, qft_out,
    win, kw, vw, awt, qf, do, wq, wk, wv, wo, q_s, dp_s, dpt_s, qft_s,
    end_send, end_recv, side_send, side_recv, corner_send, corner_recv, load_sem, store_sem,
):
    gx, gy = lax.axis_index("gx"), lax.axis_index("gy")
    loads = [
        pltpu.make_async_copy(src, dst, load_sem.at[i])
        for i, (src, dst) in enumerate(
            [(qf_in, qf), (wq_in, wq), (do_in, do), (wo_in, wo), (wk_in, wk), (wv_in, wv)]
        )
    ]
    own = pltpu.make_async_copy(anchors, win.at[1:3, 1:3], load_sem.at[6])
    for load in loads:
        load.start()
    own.start()
    greet([((gx + dx, gy + dy), inside((gx + dx, gy + dy), extents)) for dx, dy in DIRS])

    def exists(dx, dy):
        return inside((gx + dx, gy + dy), extents)

    def remote(src, dst, send, recv, dx, dy):
        return pltpu.make_async_remote_copy(
            src_ref=src, dst_ref=dst, send_sem=send, recv_sem=recv,
            device_id=(gx + dx, gy + dy), device_id_type=MESH,
        )

    def to_end(dx, c):
        n, row, goal = (0, 1, 0) if dx == 1 else (1, 0, 3)
        return remote(anchors.at[row, c], win.at[goal, c + 1], end_send.at[n, c],
                      end_recv.at[n, c], dx, 0)

    def to_side(dy):
        n, col, goal = (0, 1, 0) if dy == 1 else (1, 0, 3)
        return remote(anchors.at[:, col], win.at[1:3, goal], side_send.at[n], side_recv.at[n],
                      0, dy)

    def to_corner(dx, dy, direct):
        row, goal_row = (1, 0) if dx == 1 else (0, 3)
        col, goal_col = (1, 0) if dy == 1 else (0, 3)
        n, p = int(dx == -1), int(dy == -1)
        src = anchors.at[row, col] if direct else win.at[goal_row, col + 1]
        return remote(src, win.at[goal_row, goal_col], corner_send.at[n, p],
                      corner_recv.at[n, p], dx if direct else 0, dy)

    first = jnp.where(gy < 2, 1, 0)
    for turn in range(2):
        for dx in (1, -1):
            @pl.when(exists(dx, 0))
            def _(turn=turn, dx=dx):
                to_end(dx, first if turn == 0 else 1 - first).start()
    for dx, dy in ((1, -1), (-1, 1)):
        @pl.when(exists(dx, dy) & straight(dx, dy, gy))
        def _(dx=dx, dy=dy):
            to_corner(dx, dy, True).start()
    for dy in (1, -1):
        @pl.when(exists(0, dy))
        def _(dy=dy):
            to_side(dy).start()

    for dx, dy in DIRS:
        p0, p1 = {-1: (3, 4), 0: (1, 3), 1: (0, 1)}[dx]
        q0, q1 = {-1: (3, 4), 0: (1, 3), 1: (0, 1)}[dy]

        @pl.when(jnp.logical_not(exists(-dx, -dy)))
        def _(p0=p0, p1=p1, q0=q0, q1=q1):
            win[p0:p1, q0:q1] = jnp.zeros((p1 - p0, q1 - q0, TILE, D), BF16)

    loads[0].wait()
    loads[1].wait()

    def project_query(j, _):
        at = pl.ds(pl.multiple_of(j * 256, 256), 256)
        q_s[:, at] = (nn(qf[...], wq[:, at]).astype(BF16) * SCALE).astype(BF16)
        return 0

    lax.fori_loop(0, 3, project_query, 0)
    loads[2].wait()
    loads[3].wait()

    def project_dout(j, _):
        at = pl.ds(pl.multiple_of(j * 256, 256), 256)
        dp_s[:, at] = nt(do[...], wo[at, :]).astype(BF16)
        dpt_s[at, :] = nt(wo[at, :], do[...]).astype(BF16)
        qft_s[at, :] = qf[:, at].T
        return 0

    lax.fori_loop(0, 3, project_dout, 0)
    stores = []

    def store(src, dst):
        copy = pltpu.make_async_copy(src, dst, store_sem.at[len(stores)])
        copy.start()
        stores.append(copy)

    store(q_s, q_out)
    store(dp_s, dp_out)
    store(dpt_s, dpt_out)
    store(qft_s, qft_out)
    loads[4].wait()
    loads[5].wait()
    own.wait()

    def project_tiles(places):
        rows = jnp.concatenate([win[r, c] for r, c in places], axis=0)
        base = HELD.index(places[0])

        def step(j, _):
            at = pl.ds(pl.multiple_of(j * 256, 256), 256)
            for weight, goal in ((wk, kw), (wv, vw)):
                part = nn(rows, weight[:, at]).astype(BF16)
                for n in range(4):
                    for i in range(2):
                        goal[2 * j + i, base + n] = part[
                            n * TILE : (n + 1) * TILE, i * TILE : (i + 1) * TILE
                        ]
            return 0

        lax.fori_loop(0, 3, step, 0)
        for n, (r, c) in enumerate(places):
            awt[base + n] = win[r, c].T
        at = slice(base, base + 4)
        store(kw.at[:, at], kw_out.at[:, at])
        store(vw.at[:, at], vw_out.at[:, at])
        store(awt.at[at], awt_out.at[at])

    project_tiles(CENTRE)
    for dy in (1, -1):
        @pl.when(exists(0, -dy))
        def _(dy=dy):
            to_side(dy).wait_recv()
    project_tiles(BESIDE)
    for turn in range(2):
        for dx in (1, -1):
            c = first if turn == 0 else 1 - first

            @pl.when(exists(-dx, 0))
            def _(dx=dx, c=c):
                to_end(dx, c).wait_recv()

            for dy, col in ((1, 1), (-1, 0)):
                @pl.when(exists(-dx, 0) & exists(0, dy) & (c == col)
                         & jnp.logical_not(straight(dx, dy, gy)))
                def _(dx=dx, dy=dy):
                    to_corner(dx, dy, False).start()
    project_tiles(ENDS)
    for dx in (1, -1):
        for dy in (1, -1):
            @pl.when(exists(-dx, -dy))
            def _(dx=dx, dy=dy):
                to_corner(dx, dy, True).wait_recv()
    project_tiles(CORNERS)
    for dx in (1, -1):
        @pl.when(exists(dx, 0))
        def _(dx=dx):
            to_end(dx, 0).wait_send()
            to_end(dx, 1).wait_send()
        for dy in (1, -1):
            here = straight(dx, dy, gy)

            @pl.when(exists(dx, dy) & here | exists(-dx, dy) & jnp.logical_not(here))
            def _(dx=dx, dy=dy):
                to_corner(dx, dy, True).wait_send()
    for dy in (1, -1):
        @pl.when(exists(0, dy))
        def _(dy=dy):
            to_side(dy).wait_send()
    for copy in stores:
        copy.wait()


def halo(extents, anchors, qf, do, wq, wk, wv, wo):
    any_spec = pl.BlockSpec(memory_space=pl.ANY)
    blocks = (PAIRS, 16, TILE, TILE)
    tall, wide = (Q_DEV, D), (D, Q_DEV)
    square = (D, D)
    shapes = [blocks, blocks, (16, D, TILE), tall, tall, wide, wide]
    return pl.pallas_call(
        partial(halo_kernel, extents),
        name="halo",
        out_shape=[jax.ShapeDtypeStruct(s, BF16) for s in shapes],
        in_specs=[any_spec] * 7,
        out_specs=[any_spec] * 7,
        scratch_shapes=[
            pltpu.VMEM(s, BF16)
            for s in [(4, 4, TILE, D), blocks, blocks, (16, D, TILE), tall, tall,
                      square, square, square, square, tall, tall, wide, wide]
        ]
        + [
            pltpu.SemaphoreType.DMA(s)
            for s in [(2, 2), (2, 2), (2,), (2,), (2, 2), (2, 2), (7,), (16,)]
        ],
        compiler_params=pltpu.CompilerParams(
            collective_id=0, has_side_effects=True, vmem_limit_bytes=VMEM_BYTES
        ),
    )(anchors, qf, do, wq, wk, wv, wo)


def attention_kernel(
    lists, counts, order, kw, vw, q_ref, dp_ref, dpt_ref,
    pk_out, pv_out, att_out, dq_out, dk, dv,
):
    dk[...] = jnp.zeros_like(dk)
    dv[...] = jnp.zeros_like(dv)
    lane = lax.broadcasted_iota(jnp.int32, (TILE, TILE), 1)
    first = lane < HEAD_DIM
    for b in range(4):
        tiles = [order[lists[0, 0, b, s]] for s in range(KT)]
        count = counts[0, 0, b]
        at = slice(b * TILE, (b + 1) * TILE)
        q = q_ref[at, :]
        do = dp_ref[at, :]
        zero = jnp.zeros_like(q)
        q2 = jnp.concatenate([jnp.where(first, q, zero), jnp.where(first, zero, q)], axis=0)
        do2 = jnp.concatenate([jnp.where(first, do, zero), jnp.where(first, zero, do)], axis=0)
        keys = jnp.concatenate([kw[0, t] for t in tiles], axis=0)
        values = jnp.concatenate([vw[0, t] for t in tiles], axis=0)
        scores = nt(keys, q2)
        scores = jnp.concatenate(
            [
                scores[s * TILE : (s + 1) * TILE] + jnp.where(s < count, 0.0, NEG).astype(F32)
                for s in range(KT)
            ],
            axis=0,
        )
        top = jnp.max(scores, axis=0, keepdims=True)
        expo = jnp.exp(scores - top)
        prob = expo * (1.0 / jnp.sum(expo, axis=0, keepdims=True))
        half = prob.astype(BF16)
        att2 = tn(values, half)
        att = jnp.concatenate(
            [att2[:HEAD_DIM, :TILE], att2[HEAD_DIM:, TILE:]], axis=0
        ).astype(BF16)
        att_out[:, at] = att
        both = att.astype(F32) * dpt_ref[:, at].astype(F32)
        delta = jnp.concatenate(
            [
                jnp.sum(both[:HEAD_DIM], axis=0, keepdims=True),
                jnp.sum(both[HEAD_DIM:], axis=0, keepdims=True),
            ],
            axis=1,
        )
        dprob = nt(values, do2)
        dscore = (prob * (dprob - delta)).astype(BF16)
        dq2 = tn(keys, dscore)
        dq = jnp.concatenate([dq2[:HEAD_DIM, :TILE], dq2[HEAD_DIM:, TILE:]], axis=0) * SCALE
        dq_out[at, :] = dq.T.astype(BF16)
        dkey = nn(dscore, q2)
        dvalue = nn(half, do2)
        for s in range(KT):
            dk[tiles[s]] += dkey[s * TILE : (s + 1) * TILE]
            dv[tiles[s]] += dvalue[s * TILE : (s + 1) * TILE]
    pk_out[0] = dk[...].astype(BF16)
    pv_out[0] = dv[...].astype(BF16)


def attention(lists, counts, order, kw, vw, q, dp, dpt):
    blocks = (PAIRS, 16, TILE, TILE)
    by_pair = pl.BlockSpec((1, 16, TILE, TILE), lambda h, *_: (h, 0, 0, 0))
    tall = pl.BlockSpec((Q_DEV, TILE), lambda h, *_: (0, h))
    wide = pl.BlockSpec((TILE, Q_DEV), lambda h, *_: (h, 0))
    return pl.pallas_call(
        attention_kernel,
        name="attention",
        out_shape=[
            jax.ShapeDtypeStruct(blocks, BF16),
            jax.ShapeDtypeStruct(blocks, BF16),
            jax.ShapeDtypeStruct((D, Q_DEV), BF16),
            jax.ShapeDtypeStruct((Q_DEV, D), BF16),
        ],
        grid_spec=pltpu.PrefetchScalarGridSpec(
            num_scalar_prefetch=3,
            grid=(PAIRS,),
            in_specs=[by_pair, by_pair, tall, tall, wide],
            out_specs=[by_pair, by_pair, wide, tall],
            scratch_shapes=[pltpu.VMEM((16, TILE, TILE), F32), pltpu.VMEM((16, TILE, TILE), F32)],
        ),
        compiler_params=pltpu.CompilerParams(vmem_limit_bytes=VMEM_BYTES),
    )(lists, counts, order, kw, vw, q, dp, dpt)


def grads_kernel(
    extents,
    pk_in, pv_in, awt_in, qft_in, att_in, dq_in, do_in, wq_in, wk_in, wv_in,
    ag_out, qg_out, wg_out,
    pk, pv, awt, qft, att, dq, do, wq, wk, wv,
    corner, passed, ends, end_s, end_r, side_s, side_r, corner_r, acc, qg_s, ag_s, wg_s,
    mine, core_s, core_r, term, yf, yrl, ysum, xf, xrl, xsum,
    ta, tb, xa_r, yb_r, zs, zr, fs, fr,
    load_sem, store_sem, pass_send, pass_recv, end_send, end_recv, side_send, side_recv,
    cs_sem, cr_sem, ys_sem, yr_sem, xs_sem, xr_sem, xas_sem, xar_sem, ybs_sem, ybr_sem,
    zs_sem, zr_sem, f_sem,
):
    gx, gy = lax.axis_index("gx"), lax.axis_index("gy")
    core = lax.rem(gy, 2)
    z = lax.rem(gx, 4) * 2 + gy // 2
    x = lax.rem(gx // 4, 4)
    y = gx // 16

    def device(y, x, z, core):
        return ((y * 4 + x) * 4 + z // 2, lax.rem(z, 2) * 2 + core)

    def exists(dx, dy):
        return inside((gx + dx, gy + dy), extents)

    groups = [slice(12, 16), slice(8, 12), slice(4, 8), slice(0, 4)]
    pairs = [(wk_in, wk), (wv_in, wv)]
    for at in groups:
        pairs += [(pk_in.at[:, at], pk.at[:, at]), (pv_in.at[:, at], pv.at[:, at])]
    pairs += [(qft_in, qft), (dq_in, dq), (att_in, att), (do_in, do), (awt_in, awt), (wq_in, wq)]
    loads = [pltpu.make_async_copy(s, d, load_sem.at[i]) for i, (s, d) in enumerate(pairs)]
    for load in loads:
        load.start()
    sibling = device(y, x, z, 1 - core)
    fixed = [sibling]
    fixed += [device(lax.rem(y + k, 4), x, z, core) for k in (1, 2, 3)]
    fixed += [device(y, lax.rem(x + k, 4), z, core) for k in (1, 2, 3)]
    fixed += [device(y, x, lax.rem(z + k, 8), core) for k in range(1, 8)]
    greet([((gx + dx, gy + dy), exists(dx, dy)) for dx, dy in DIRS]
          + [(where, gx >= 0) for where in fixed])

    def remote(src, dst, send, recv, where):
        return pltpu.make_async_remote_copy(
            src_ref=src, dst_ref=dst, send_sem=send, recv_sem=recv,
            device_id=where, device_id_type=MESH,
        )

    def terms_of(group, goal):
        base = 4 * group

        def side(blocks):
            return jnp.concatenate(
                [blocks[h, base : base + 4].reshape(4 * TILE, TILE) for h in range(PAIRS)], axis=1
            )

        left_k, left_v = side(pk), side(pv)

        def step(j, _):
            at = pl.ds(pl.multiple_of(j * 256, 256), 256)
            part = nt(left_k, wk[at, :]) + nt(left_v, wv[at, :])
            for n in range(4):
                goal[n, :, at] = part[n * TILE : (n + 1) * TILE].astype(goal.dtype)
            return 0

        lax.fori_loop(0, 3, step, 0)

    def from_corner(rx, ry, direct):
        n, p = int(rx == 1), int(ry == 1)
        dst = corner_r.at[n] if direct else passed.at[n, 1 - p]
        return remote(corner.at[2 * n + p], dst, pass_send.at[n, p], pass_recv.at[n, 1 - p],
                      (gx + (rx if direct else 0), gy + ry))

    def from_end(rx, c):
        n = int(rx == 1)
        return remote(end_s.at[2 * n + c], end_r.at[n, c], end_send.at[n, c], end_recv.at[n, c],
                      (gx + rx, gy))

    def from_side(ry):
        p = int(ry == 1)
        return remote(side_s.at[2 * p : 2 * p + 2], side_r.at[p], side_send.at[p],
                      side_recv.at[p], (gx, gy + ry))

    for load in loads[0:4]:
        load.wait()
    terms_of(3, corner)
    for rx, ry in ((-1, 1), (1, -1), (-1, -1), (1, 1)):
        direct = straight(-rx, -ry, gy + ry)

        @pl.when(exists(rx, ry) & direct)
        def _(rx=rx, ry=ry):
            from_corner(rx, ry, True).start()

        @pl.when(exists(rx, ry) & jnp.logical_not(direct))
        def _(rx=rx, ry=ry):
            from_corner(rx, ry, False).start()
    for load in loads[4:6]:
        load.wait()
    terms_of(2, ends)
    for load in loads[6:8]:
        load.wait()
    terms_of(1, side_s)
    first = jnp.where(gy < 2, 0, 1)
    for turn in range(2):
        c = first if turn == 0 else 1 - first
        for rx in (-1, 1):
            n = int(rx == 1)
            waits = jnp.where(
                c == 0,
                exists(rx, -1) & jnp.logical_not(straight(-rx, -1, gy)),
                exists(rx, 1) & jnp.logical_not(straight(-rx, 1, gy)),
            )

            @pl.when(exists(rx, 0) & waits)
            def _(rx=rx, n=n, c=c):
                remote(corner.at[0], passed.at[n, c], pass_send.at[0, 0], pass_recv.at[n, c],
                       sibling).wait_recv()
                end_s[2 * n + c] = (ends[2 * n + c] + passed[n, c].astype(F32)).astype(BF16)

            @pl.when(exists(rx, 0) & jnp.logical_not(waits))
            def _(n=n, c=c):
                end_s[2 * n + c] = ends[2 * n + c].astype(BF16)

            @pl.when(exists(rx, 0))
            def _(rx=rx, c=c):
                from_end(rx, c).start()
    for ry in (-1, 1):
        @pl.when(exists(0, ry))
        def _(ry=ry):
            from_side(ry).start()

    def crossing(m):
        return remote(core_s.at[m], core_r.at[m], cs_sem.at[m], cr_sem.at[m], sibling)

    def weight_halves(m, rows_of, columns_of):
        def step(n, _):
            half = jnp.where(n == 0, 1 - core, core)
            part = nn(rows_of(), columns_of(half))

            @pl.when(n == 0)
            def _():
                core_s[m] = part.astype(BF16)
                crossing(m).start()

            @pl.when(n == 1)
            def _():
                mine[m] = part
            return 0

        lax.fori_loop(0, 2, step, 0)

    y_up, y_down = device(lax.rem(y + 1, 4), x, z, core), device(lax.rem(y + 3, 4), x, z, core)
    x_next, x_over, x_last = lax.rem(x + 1, 4), lax.rem(x + 2, 4), lax.rem(x + 3, 4)
    x_up, x_down = device(y, x_next, z, core), device(y, x_last, z, core)

    def y_copy(m, i):
        low, high = slice(0, 2), slice(2, 4)
        src, dst, where = [
            (term.at[m, high, 0], yf.at[0, high], y_up),
            (term.at[m, low, 0], yf.at[1, low], y_down),
            (term.at[m, low, 0], yrl.at[0], y_up),
            (term.at[m, high, 0], yrl.at[1], y_down),
            (ysum.at[0], yf.at[0, low], y_up),
            (ysum.at[1], yf.at[1, high], y_down),
        ][i]
        return remote(src, dst, ys_sem.at[i], yr_sem.at[i], where)

    def x_copy(m, i):
        low, high = slice(0, 48), slice(48, 96)
        src, dst, where = [
            (term.at[m, x_next, 1, high], xf.at[m, 0, high], x_up),
            (term.at[m, x_last, 1, low], xf.at[m, 1, low], x_down),
            (term.at[m, x_over, 1, low], xrl.at[m, 0], x_up),
            (term.at[m, x_over, 1, high], xrl.at[m, 1], x_down),
            (xsum.at[m, 0], xf.at[m, 0, low], x_up),
            (xsum.at[m, 1], xf.at[m, 1, high], x_down),
        ][i]
        return remote(src, dst, xs_sem.at[m, i], xr_sem.at[m, i], where)

    def y_place(m):
        return lax.rem(m - y + 4, 4)

    def add_cores(m):
        crossing(m).wait()
        for goal in range(4):
            for part in range(2):
                at = slice(goal * 192 + part * 96, goal * 192 + part * 96 + 96)
                term[m, goal, part] = (mine[m, at] + core_r[m, at].astype(F32)).astype(BF16)

        @pl.when(y_place(m) == 2)
        def _():
            y_copy(m, 2).start()
            y_copy(m, 3).start()

        for i in (2, 3):
            x_copy(m, i).start()

        @pl.when(y_place(m) == 1)
        def _():
            y_copy(m, 0).start()

        @pl.when(y_place(m) == 3)
        def _():
            y_copy(m, 1).start()

        for i in (0, 1):
            x_copy(m, i).start()

    def hand_on(m):
        @pl.when(y_place(m) == 1)
        def _():
            y_copy(m, 2).wait_recv()
            for goal in range(2):
                ysum[0, goal] = (
                    term[m, goal, 0].astype(F32) + yrl[0, goal].astype(F32)
                ).astype(BF16)
            y_copy(m, 4).start()

        @pl.when(y_place(m) == 3)
        def _():
            y_copy(m, 3).wait_recv()
            for goal in range(2):
                ysum[1, goal] = (
                    term[m, 2 + goal, 0].astype(F32) + yrl[1, goal].astype(F32)
                ).astype(BF16)
            y_copy(m, 5).start()

        for n, goal in ((0, x_next), (1, x_last)):
            x_copy(m, 2 + n).wait_recv()
            at = slice(48 * n, 48 * n + 48)
            xsum[m, n] = (
                term[m, goal, 1, at].astype(F32) + xrl[m, n].astype(F32)
            ).astype(BF16)
            x_copy(m, 4 + n).start()

    def lanes(ref, half):
        return ref[:, pl.ds(pl.multiple_of(half * HALF, 128), HALF)]

    def stacked(ref, half):
        return jnp.concatenate(
            [ref[half * 3 + i].reshape(16 * TILE, TILE) for i in range(3)], axis=1
        )

    def anchor_rows():
        return jnp.concatenate([awt[t] for t in range(16)], axis=1)

    for load in loads[10:14]:
        load.wait()
    weight_halves(0, lambda: qft[...], lambda half: lanes(dq, half))
    weight_halves(3, lambda: att[...], lambda half: lanes(do, half))
    add_cores(0)
    for load in loads[8:10] + loads[14:15]:
        load.wait()
    weight_halves(1, anchor_rows, lambda half: stacked(pk, half))
    add_cores(3)
    hand_on(0)
    weight_halves(2, anchor_rows, lambda half: stacked(pv, half))
    add_cores(1)
    hand_on(3)
    add_cores(2)

    terms_of(0, acc)
    hand_on(1)
    loads[15].wait()

    def query_grad(j, _):
        at = pl.ds(pl.multiple_of(j * 256, 256), 256)
        qg_s[:, at] = nt(dq[...], wq[at, :]).astype(BF16)
        return 0

    lax.fori_loop(0, 3, query_grad, 0)
    qg_copy = pltpu.make_async_copy(qg_s, qg_out, store_sem.at[0])
    qg_copy.start()
    hand_on(2)

    for i in (0, 1, 4, 5):
        y_copy(0, i).wait_recv()
    for goal in range(4):
        total = term[y, goal, 0].astype(F32)
        ta[goal] = (total + yf[0, goal].astype(F32) + yf[1, goal].astype(F32)).astype(BF16)

    def to_column_second(k):
        goal = lax.rem(x + k, 4)
        return remote(ta.at[goal], xa_r.at[3 - k], xas_sem.at[k - 1], xar_sem.at[3 - k],
                      device(y, goal, z, core))

    for k in (2, 1, 3):
        to_column_second(k).start()
    for m in range(4):
        for i in (0, 1, 4, 5):
            x_copy(m, i).wait_recv()
        total = term[m, x, 1].astype(F32)
        tb[m] = (total + xf[m, 0].astype(F32) + xf[m, 1].astype(F32)).astype(BF16)

    def to_row_second(k):
        goal = lax.rem(y + k, 4)
        return remote(tb.at[goal], yb_r.at[3 - k], ybs_sem.at[k - 1], ybr_sem.at[3 - k],
                      device(goal, x, z, core))

    for k in (2, 1, 3):
        to_row_second(k).start()

    zs[:, 16:32] = jnp.zeros((8, 16, HALF), BF16)
    for k in (1, 2, 3):
        to_column_second(k).wait_recv()
    total = ta[x].astype(F32)
    for slot in range(3):
        total = total + xa_r[slot].astype(F32)
    for i in range(4):
        zs[i, 0:24] = total[i * 24 : (i + 1) * 24].astype(BF16)
    for k in (1, 2, 3):
        to_row_second(k).wait_recv()
    total = tb[y].astype(F32)
    for slot in range(3):
        total = total + yb_r[slot].astype(F32)
    for i in range(4):
        zs[4 + i, 0:24] = total[i * 24 : (i + 1) * 24].astype(BF16)

    def along(k):
        goal = lax.rem(z + k, 8)
        return remote(zs.at[goal], zr.at[7 - k], zs_sem.at[k - 1], zr_sem.at[7 - k],
                      device(y, x, goal, core))

    for k in (4, 3, 5, 2, 6, 1, 7):
        along(k).start()

    for ry in (-1, 1):
        @pl.when(exists(0, -ry))
        def _(ry=ry):
            from_side(ry).wait_recv()
            p, c = (1, 0) if ry == 1 else (0, 1)
            for r in range(2):
                acc[2 * r + c] += side_r[p, r].astype(F32)
    for rx in (-1, 1):
        n, r = (1, 0) if rx == 1 else (0, 1)

        @pl.when(exists(-rx, 0))
        def _(rx=rx, n=n, r=r):
            for c in range(2):
                from_end(rx, c).wait_recv()
                acc[2 * r + c] += end_r[n, c].astype(F32)
    for rx, ry in ((-1, 1), (1, -1)):
        n, r = (1, 0) if rx == 1 else (0, 1)
        p, c = (1, 0) if ry == 1 else (0, 1)

        @pl.when(exists(-rx, -ry) & straight(-rx, -ry, gy))
        def _(rx=rx, ry=ry, n=n, p=p, r=r, c=c):
            remote(corner.at[0], corner_r.at[n], pass_send.at[0, 0], pass_recv.at[n, 1 - p],
                   sibling).wait_recv()
            acc[2 * r + c] += corner_r[n].astype(F32)

    ag_s[...] = acc[...].astype(BF16)
    ag_copy = pltpu.make_async_copy(ag_s, ag_out, store_sem.at[1])
    ag_copy.start()

    for k in range(1, 8):
        along(k).wait_recv()
    total = zs[z].astype(F32)
    for slot in range(7):
        total = total + zr[slot].astype(F32)
    fs[...] = total[0:24]
    last = remote(fs, fr, f_sem.at[0], f_sem.at[1], sibling)
    last.start()
    last.wait()
    low = core == 0
    held, other = fs[...], fr[...]
    held = jnp.where(low, held[0:12], held[12:24])
    other = jnp.where(low, other[0:12], other[12:24])
    norm = (extents[0] * extents[1] * Q_DEV) ** (-0.5)
    wg_s[:, 0:HALF] = jnp.where(low, held, other) * norm
    wg_s[:, HALF:D] = jnp.where(low, other, held) * norm
    wg_copy = pltpu.make_async_copy(wg_s, wg_out, store_sem.at[2])
    wg_copy.start()

    for rx in (-1, 1):
        @pl.when(exists(rx, 0))
        def _(rx=rx):
            from_end(rx, 0).wait_send()
            from_end(rx, 1).wait_send()
        for ry in (-1, 1):
            @pl.when(exists(rx, ry))
            def _(rx=rx, ry=ry):
                from_corner(rx, ry, False).wait_send()
    for ry in (-1, 1):
        @pl.when(exists(0, ry))
        def _(ry=ry):
            from_side(ry).wait_send()
    for i in range(6):
        y_copy(0, i).wait_send()
    for m in range(4):
        for i in range(6):
            x_copy(m, i).wait_send()
    for k in (1, 2, 3):
        to_column_second(k).wait_send()
        to_row_second(k).wait_send()
    for k in range(1, 8):
        along(k).wait_send()
    qg_copy.wait()
    ag_copy.wait()
    wg_copy.wait()


def grads(extents, pk, pv, awt, qft, att, dq, do, wq, wk, wv):
    any_spec = pl.BlockSpec(memory_space=pl.ANY)
    blocks = (PAIRS, 16, TILE, TILE)
    tall, wide, square = (Q_DEV, D), (D, Q_DEV), (D, D)
    four, two = (4, TILE, D), (2, 2, TILE, D)
    dma = pltpu.SemaphoreType.DMA
    held = [
        (blocks, BF16), (blocks, BF16), ((16, D, TILE), BF16), (wide, BF16), (wide, BF16),
        (tall, BF16), (tall, BF16), (square, BF16), (square, BF16), (square, BF16),
        (four, BF16), (two, BF16), (four, F32), (four, BF16), (two, BF16), (four, BF16),
        (two, BF16), ((2, TILE, D), BF16), (four, F32), (tall, BF16), (four, BF16),
        ((12, D), F32),
        ((4, D, HALF), F32), ((4, D, HALF), BF16), ((4, D, HALF), BF16),
        ((4, 4, 2, 96, HALF), BF16),
        ((2, 4, 96, HALF), BF16), ((2, 2, 96, HALF), BF16), ((2, 2, 96, HALF), BF16),
        ((4, 2, 96, HALF), BF16), ((4, 2, 48, HALF), BF16), ((4, 2, 48, HALF), BF16),
        ((4, 96, HALF), BF16), ((4, 96, HALF), BF16), ((3, 96, HALF), BF16),
        ((3, 96, HALF), BF16), ((8, 32, HALF), BF16), ((7, 32, HALF), BF16),
        ((24, HALF), F32), ((24, HALF), F32),
    ]
    sems = [(16,), (3,), (2, 2), (2, 2), (2, 2), (2, 2), (2,), (2,), (4,), (4,), (6,), (6,),
            (4, 6), (4, 6), (3,), (3,), (3,), (3,), (7,), (7,), (2,)]
    anchor_grad, query_grad, weight_grads = pl.pallas_call(
        partial(grads_kernel, extents),
        name="grads",
        out_shape=[
            jax.ShapeDtypeStruct(four, BF16),
            jax.ShapeDtypeStruct(tall, BF16),
            jax.ShapeDtypeStruct((12, D), F32),
        ],
        in_specs=[any_spec] * 10,
        out_specs=[any_spec] * 3,
        scratch_shapes=[pltpu.VMEM(s, t) for s, t in held] + [dma(s) for s in sems],
        compiler_params=pltpu.CompilerParams(
            collective_id=1, has_side_effects=True, vmem_limit_bytes=VMEM_BYTES
        ),
    )(pk, pv, awt, qft, att, dq, do, wq, wk, wv)
    return anchor_grad.reshape(2, 2, TILE, D), query_grad, weight_grads


def on_device(
    extents,
    query_feats, anchors, tile_lists, tile_counts, out_grad, w_query, w_key, w_value, w_out,
):
    qf = query_feats.reshape(Q_DEV, D)
    do = out_grad.reshape(Q_DEV, D)
    order = jnp.array([HELD.index((w // 4, w % 4)) for w in range(16)], jnp.int32)
    kw, vw, awt, q, dp, dpt, qft = halo(extents, anchors, qf, do, w_query, w_key, w_value, w_out)
    pk, pv, att, dq = attention(tile_lists, tile_counts, order, kw, vw, q, dp, dpt)
    anchor_grad, query_grad, weight_grads = grads(
        extents, pk, pv, awt, qft, att, dq, do, w_query, w_key, w_value
    )
    return query_grad.reshape(query_feats.shape), anchor_grad, weight_grads


def solution(mesh):
    four = P("gx", "gy", None, None)
    in_specs = (four, four, four, P("gx", "gy", None), four, P(), P(), P(), P())
    out_specs = (four, four, P(("gx", "gy"), None))
    extents = (mesh.shape["gx"], mesh.shape["gy"])
    return jax.shard_map(
        partial(on_device, extents),
        mesh=mesh, in_specs=in_specs, out_specs=out_specs, check_vma=False,
    )
```

```python
from functools import partial

import jax
import jax.numpy as jnp
from jax import lax
from jax.experimental import pallas as pl
from jax.experimental.pallas import tpu as pltpu
from jax.sharding import PartitionSpec as P

HEADS = 12
HEAD_DIM = 64
KT = 4
D = 768
TILE = 128
PAIRS = 6
Q_DEV = 512
SCALE = HEAD_DIM ** (-0.5)
HALF = 384
LOG2E = 1.4426950408889634
DEAD = 1e30
ORDER = (
    "X", "C", "A0", "B0", "A1", "B1", "E", "A2", "B2", "A3", "B3", "G", "H0", "H1", "S", "H2", "H3",
    "K",
)
MESH = pl.DeviceIdType.MESH
F32 = jnp.float32
BF16 = jnp.bfloat16
PIECES = ("q", "0", "1", "2", "o", "")
VMEM_BYTES = 56 * 1024 * 1024

DIRS = ((-1, 0), (1, 0), (-1, -1), (-1, 1), (1, -1), (1, 1), (0, -1), (0, 1))
CENTRE = ((1, 1), (1, 2), (2, 1), (2, 2))
BESIDE = ((1, 0), (2, 0), (1, 3), (2, 3))
ENDS = ((0, 1), (0, 2), (3, 1), (3, 2))
CORNERS = ((0, 0), (3, 0), (0, 3), (3, 3))
HELD = CENTRE + BESIDE + ENDS + CORNERS


def nn(left, right):
    return lax.dot_general(left, right, (((1,), (0,)), ((), ())), preferred_element_type=F32)


def nt(left, right):
    return lax.dot_general(left, right, (((1,), (1,)), ((), ())), preferred_element_type=F32)


def tn(left, right):
    return lax.dot_general(left, right, (((0,), (0,)), ((), ())), preferred_element_type=F32)


def inside(place, extents):
    (px, py), (nx, ny) = place, extents
    return (px >= 0) & (px < nx) & (py >= 0) & (py < ny)


def greet(partners):
    barrier = pltpu.get_barrier_semaphore()
    total = jnp.int32(0)
    for where, present in partners:
        @pl.when(present)
        def _():
            pl.semaphore_signal(barrier, inc=1, device_id=where, device_id_type=MESH)
        total = total + jnp.where(present, 1, 0).astype(jnp.int32)
    pl.semaphore_wait(barrier, total)


def straight(dx, dy, gy):
    return ((dx, dy) == (1, -1)) & (gy == 2) | ((dx, dy) == (-1, 1)) & (gy == 1)


def halo_kernel(
    extents,
    anchors, qf_in, do_in, wq_in, wk_in, wv_in, wo_in,
    kw_out, vw_out, awt_out, q_out, dp_out, dpt_out, qft_out,
    win, kw, vw, awt, qf, do, wq, wk, wv, wo, q_s, dp_s, dpt_s, qft_s,
    end_send, end_recv, side_send, side_recv, corner_send, corner_recv, load_sem, store_sem,
):
    gx, gy = lax.axis_index("gx"), lax.axis_index("gy")
    loads = [
        pltpu.make_async_copy(src, dst, load_sem.at[i])
        for i, (src, dst) in enumerate(
            [(qf_in, qf), (wq_in, wq), (do_in, do), (wo_in, wo), (wk_in, wk), (wv_in, wv)]
        )
    ]
    own = pltpu.make_async_copy(anchors, win.at[1:3, 1:3], load_sem.at[6])
    for load in loads:
        load.start()
    own.start()
    greet([((gx + dx, gy + dy), inside((gx + dx, gy + dy), extents)) for dx, dy in DIRS])

    def exists(dx, dy):
        return inside((gx + dx, gy + dy), extents)

    def remote(src, dst, send, recv, dx, dy):
        return pltpu.make_async_remote_copy(
            src_ref=src, dst_ref=dst, send_sem=send, recv_sem=recv,
            device_id=(gx + dx, gy + dy), device_id_type=MESH,
        )

    def to_end(dx, c):
        n, row, goal = (0, 1, 0) if dx == 1 else (1, 0, 3)
        return remote(anchors.at[row, c], win.at[goal, c + 1], end_send.at[n, c],
                      end_recv.at[n, c], dx, 0)

    def to_side(dy):
        n, col, goal = (0, 1, 0) if dy == 1 else (1, 0, 3)
        return remote(anchors.at[:, col], win.at[1:3, goal], side_send.at[n], side_recv.at[n],
                      0, dy)

    def to_corner(dx, dy, direct):
        row, goal_row = (1, 0) if dx == 1 else (0, 3)
        col, goal_col = (1, 0) if dy == 1 else (0, 3)
        n, p = int(dx == -1), int(dy == -1)
        src = anchors.at[row, col] if direct else win.at[goal_row, col + 1]
        return remote(src, win.at[goal_row, goal_col], corner_send.at[n, p],
                      corner_recv.at[n, p], dx if direct else 0, dy)

    first = jnp.where(gy < 2, 1, 0)
    for turn in range(2):
        for dx in (1, -1):
            @pl.when(exists(dx, 0))
            def _(turn=turn, dx=dx):
                to_end(dx, first if turn == 0 else 1 - first).start()
    for dx, dy in ((1, -1), (-1, 1)):
        @pl.when(exists(dx, dy) & straight(dx, dy, gy))
        def _(dx=dx, dy=dy):
            to_corner(dx, dy, True).start()
    for dy in (1, -1):
        @pl.when(exists(0, dy))
        def _(dy=dy):
            to_side(dy).start()

    for dx, dy in DIRS:
        p0, p1 = {-1: (3, 4), 0: (1, 3), 1: (0, 1)}[dx]
        q0, q1 = {-1: (3, 4), 0: (1, 3), 1: (0, 1)}[dy]

        @pl.when(jnp.logical_not(exists(-dx, -dy)))
        def _(p0=p0, p1=p1, q0=q0, q1=q1):
            win[p0:p1, q0:q1] = jnp.zeros((p1 - p0, q1 - q0, TILE, D), BF16)

    loads[0].wait()
    loads[1].wait()

    def project_query(j, _):
        at = pl.ds(pl.multiple_of(j * 256, 256), 256)
        q_s[:, at] = (nn(qf[...], wq[:, at]).astype(BF16) * SCALE).astype(BF16)
        return 0

    lax.fori_loop(0, 3, project_query, 0)
    loads[2].wait()
    loads[3].wait()

    def project_dout(j, _):
        at = pl.ds(pl.multiple_of(j * 256, 256), 256)
        dp_s[:, at] = nt(do[...], wo[at, :]).astype(BF16)
        dpt_s[at, :] = nt(wo[at, :], do[...]).astype(BF16)
        qft_s[at, :] = qf[:, at].T
        return 0

    lax.fori_loop(0, 3, project_dout, 0)
    stores = []

    def store(src, dst):
        copy = pltpu.make_async_copy(src, dst, store_sem.at[len(stores)])
        copy.start()
        stores.append(copy)

    store(q_s, q_out)
    store(dp_s, dp_out)
    store(dpt_s, dpt_out)
    store(qft_s, qft_out)
    loads[4].wait()
    loads[5].wait()
    own.wait()

    def project_tiles(places, base):
        rows = jnp.concatenate([win[r, c] for r, c in places], axis=0)
        count = len(places)

        def step(j, _):
            at = pl.ds(pl.multiple_of(j * 256, 256), 256)
            for weight, goal in ((wk, kw), (wv, vw)):
                part = nn(rows, weight[:, at]).astype(BF16)
                for n in range(count):
                    for i in range(2):
                        goal[2 * j + i, base + n] = part[
                            n * TILE : (n + 1) * TILE, i * TILE : (i + 1) * TILE
                        ]
            return 0

        lax.fori_loop(0, 3, step, 0)
        for n, (r, c) in enumerate(places):
            awt[:, pl.ds(pl.multiple_of((base + n) * TILE, TILE), TILE)] = win[r, c].T
        at = pl.ds(base, count)
        wide = pl.ds(pl.multiple_of(base * TILE, TILE), count * TILE)
        store(kw.at[:, at], kw_out.at[:, at])
        store(vw.at[:, at], vw_out.at[:, at])
        store(awt.at[:, wide], awt_out.at[:, wide])

    project_tiles(CENTRE, 0)
    for dy in (1, -1):
        @pl.when(exists(0, -dy))
        def _(dy=dy):
            to_side(dy).wait_recv()
    project_tiles(BESIDE, 4)
    for turn in range(2):
        for dx in (1, -1):
            c = first if turn == 0 else 1 - first

            @pl.when(exists(-dx, 0))
            def _(dx=dx, c=c):
                to_end(dx, c).wait_recv()

            for dy, col in ((1, 1), (-1, 0)):
                @pl.when(exists(-dx, 0) & exists(0, dy) & (c == col)
                         & jnp.logical_not(straight(dx, dy, gy)))
                def _(dx=dx, dy=dy):
                    to_corner(dx, dy, False).start()
    project_tiles(ENDS, 8)
    for turn in range(2):
        side = lax.rem(gy + 1 + turn, 2)
        for dy, p in ((1, 0), (-1, 1)):
            for dx in (1, -1):
                @pl.when(exists(-dx, -dy) & (side == p))
                def _(dx=dx, dy=dy):
                    to_corner(dx, dy, True).wait_recv()
        project_tiles([(0, 3 * side), (3, 3 * side)], 12 + 2 * side)
    for dx in (1, -1):
        @pl.when(exists(dx, 0))
        def _(dx=dx):
            to_end(dx, 0).wait_send()
            to_end(dx, 1).wait_send()
        for dy in (1, -1):
            here = straight(dx, dy, gy)

            @pl.when(exists(dx, dy) & here | exists(-dx, dy) & jnp.logical_not(here))
            def _(dx=dx, dy=dy):
                to_corner(dx, dy, True).wait_send()
    for dy in (1, -1):
        @pl.when(exists(0, dy))
        def _(dy=dy):
            to_side(dy).wait_send()
    for copy in stores:
        copy.wait()


def halo(extents, anchors, qf, do, wq, wk, wv, wo):
    any_spec = pl.BlockSpec(memory_space=pl.ANY)
    blocks = (PAIRS, 16, TILE, TILE)
    tall, wide = (Q_DEV, D), (D, Q_DEV)
    square = (D, D)
    shapes = [blocks, blocks, (D, 16 * TILE), tall, tall, wide, wide]
    return pl.pallas_call(
        partial(halo_kernel, extents),
        name="halo",
        out_shape=[jax.ShapeDtypeStruct(s, BF16) for s in shapes],
        in_specs=[any_spec] * 7,
        out_specs=[any_spec] * 7,
        scratch_shapes=[
            pltpu.VMEM(s, BF16)
            for s in [(4, 4, TILE, D), blocks, blocks, (D, 16 * TILE), tall, tall,
                      square, square, square, square, tall, tall, wide, wide]
        ]
        + [
            pltpu.SemaphoreType.DMA(s)
            for s in [(2, 2), (2, 2), (2,), (2,), (2, 2), (2, 2), (7,), (19,)]
        ],
        compiler_params=pltpu.CompilerParams(
            collective_id=0, has_side_effects=True, vmem_limit_bytes=VMEM_BYTES
        ),
    )(anchors, qf, do, wq, wk, wv, wo)


def attention_kernel(
    lists, counts, order, kw, vw, q_ref, dp_ref, dpt_ref, awt_in, qft_in, do_in, wq_in,
    pk_out, pv_out, w_out, wo_out, qg_out,
    dk, dv, kv, att_s, dq_s, awt, qft, do_s, wq, sem,
):
    pair = pl.program_id(0)
    loads = [
        pltpu.make_async_copy(src, dst, sem.at[i])
        for i, (src, dst) in enumerate([(qft_in, qft), (do_in, do_s), (awt_in, awt), (wq_in, wq)])
    ]

    @pl.when(pair == 0)
    def _():
        for load in loads:
            load.start()

    slot, last = lax.rem(pair, 2), lax.rem(pair + 1, 2)

    def kept(which):
        return pl.ds(pl.multiple_of(which * TILE, TILE), TILE)

    before = kept(jnp.maximum(pair - 1, 0))

    def pair_weights(i):
        at = slice(i * 256, (i + 1) * 256)
        both = nn(awt[at, :], kv[last]).astype(BF16)
        w_out[0, 1, at, :] = both[:, :TILE]
        w_out[0, 2, at, :] = both[:, TILE:]

    def query_weights():
        w_out[0, 0] = nn(qft[...], dq_s[:, before]).astype(BF16)

    def out_weights():
        wo_out[...] = nn(att_s[last], do_s[...]).astype(BF16)

    first = lax.broadcasted_iota(jnp.int32, (TILE, TILE), 1) < HEAD_DIM

    def products(b):
        tiles = [order[lists[0, 0, b, s]] for s in range(KT)]
        at = slice(b * TILE, (b + 1) * TILE)
        q, do = q_ref[at, :], dp_ref[at, :]
        zero = jnp.zeros_like(q)
        q2 = jnp.concatenate([jnp.where(first, q, zero), jnp.where(first, zero, q)], axis=0)
        do2 = jnp.concatenate([jnp.where(first, do, zero), jnp.where(first, zero, do)], axis=0)
        keys = jnp.concatenate([kw[0, t] for t in tiles], axis=0)
        values = jnp.concatenate([vw[0, t] for t in tiles], axis=0)
        return b, at, tiles, q2, do2, keys, values, nt(keys, q2), nt(values, do2)

    def softmax(state):
        b, at, tiles, q2, do2, keys, values, scores, dprob = state
        live = [s < counts[0, 0, b] for s in range(KT)]
        slots = [scores[s * TILE : (s + 1) * TILE] for s in range(KT)]
        top = jnp.max(slots[0], axis=0, keepdims=True)
        for s in range(1, KT):
            best = jnp.max(slots[s], axis=0, keepdims=True)
            top = jnp.maximum(top, jnp.where(live[s], best, -jnp.inf))
        top = top * LOG2E
        expo = jnp.concatenate(
            [
                jnp.exp2(slots[s] * LOG2E - (top + jnp.where(live[s], 0.0, DEAD).astype(F32)))
                for s in range(KT)
            ],
            axis=0,
        )
        prob = expo * (1.0 / jnp.sum(expo, axis=0, keepdims=True))
        half = prob.astype(BF16)
        att2 = tn(values, half)
        att = jnp.concatenate(
            [att2[:HEAD_DIM, :TILE], att2[HEAD_DIM:, TILE:]], axis=0
        ).astype(BF16)
        att_s[slot, :, at] = att
        both = att.astype(F32) * dpt_ref[:, at].astype(F32)
        delta = jnp.concatenate(
            [
                jnp.sum(both[:HEAD_DIM], axis=0, keepdims=True),
                jnp.sum(both[HEAD_DIM:], axis=0, keepdims=True),
            ],
            axis=1,
        )
        return at, tiles, q2, do2, keys, half, (prob * (dprob - delta)).astype(BF16)

    def gradients(state):
        at, tiles, q2, do2, keys, half, dscore = state
        dq2 = tn(keys, dscore)
        dq = jnp.concatenate([dq2[:HEAD_DIM, :TILE], dq2[HEAD_DIM:, TILE:]], axis=0) * SCALE
        dq_s[at, kept(pair)] = dq.T.astype(BF16)
        dkey = nn(dscore, q2)
        dvalue = nn(half, do2)
        for s in range(KT):
            dk[tiles[s]] += dkey[s * TILE : (s + 1) * TILE]
            dv[tiles[s]] += dvalue[s * TILE : (s + 1) * TILE]

    def all_blocks(weights):
        dk[...] = jnp.zeros_like(dk)
        dv[...] = jnp.zeros_like(dv)
        ahead, behind = {}, {}
        for turn in range(6):
            if turn < 4:
                ahead[turn] = products(turn)
            if 1 <= turn < 5:
                behind[turn - 1] = softmax(ahead.pop(turn - 1))
            if weights:
                for piece in PIECES[turn].split():
                    if piece == "q":
                        query_weights()
                    elif piece == "o":
                        out_weights()
                    else:
                        pair_weights(int(piece))
            if turn >= 2:
                gradients(behind.pop(turn - 2))
        for t in range(16):
            key_part, value_part = dk[t].astype(BF16), dv[t].astype(BF16)
            pk_out[0, t] = key_part
            pv_out[0, t] = value_part
            kv[slot, t * TILE : (t + 1) * TILE, :TILE] = key_part
            kv[slot, t * TILE : (t + 1) * TILE, TILE:] = value_part

    @pl.when(pair == 0)
    def _():
        all_blocks(False)
        for load in loads:
            load.wait()

    @pl.when((pair > 0) & (pair < PAIRS))
    def _():
        all_blocks(True)

    @pl.when(pair == PAIRS)
    def _():
        out_weights()
        query_weights()
        for i in range(3):
            pair_weights(i)
        for i in range(3):
            at = slice(i * 256, (i + 1) * 256)
            qg_out[:, at] = nt(dq_s[...], wq[at, :]).astype(BF16)


def attention(lists, counts, order, kw, vw, q, dp, dpt, awt, qft, do, wq):
    blocks = (PAIRS, 16, TILE, TILE)
    here = lambda p: jnp.minimum(p, PAIRS - 1)
    past = lambda p: jnp.maximum(p - 1, 0)
    by_pair = pl.BlockSpec((1, 16, TILE, TILE), lambda p, *_: (here(p), 0, 0, 0))
    tall = pl.BlockSpec((Q_DEV, TILE), lambda p, *_: (0, here(p)))
    wide = pl.BlockSpec((TILE, Q_DEV), lambda p, *_: (here(p), 0))
    any_spec = pl.BlockSpec(memory_space=pl.ANY)
    vmem = pltpu.VMEM
    return pl.pallas_call(
        attention_kernel,
        name="attention",
        out_shape=[
            jax.ShapeDtypeStruct(blocks, BF16),
            jax.ShapeDtypeStruct(blocks, BF16),
            jax.ShapeDtypeStruct((2, 3, D, HALF), BF16),
            jax.ShapeDtypeStruct((D, D), BF16),
            jax.ShapeDtypeStruct((Q_DEV, D), BF16),
        ],
        grid_spec=pltpu.PrefetchScalarGridSpec(
            num_scalar_prefetch=3,
            grid=(PAIRS + 1,),
            in_specs=[by_pair, by_pair, tall, tall, wide] + [any_spec] * 4,
            out_specs=[
                by_pair,
                by_pair,
                pl.BlockSpec((1, 3, D, TILE), lambda p, *_: (past(p) // 3, 0, 0, past(p) % 3)),
                pl.BlockSpec((TILE, D), lambda p, *_: (past(p), 0)),
                pl.BlockSpec((Q_DEV, D), lambda p, *_: (0, 0)),
            ],
            scratch_shapes=[
                vmem((16, TILE, TILE), F32), vmem((16, TILE, TILE), F32),
                vmem((2, 16 * TILE, 2 * TILE), BF16), vmem((2, TILE, Q_DEV), BF16),
                vmem((Q_DEV, D), BF16), vmem((D, 16 * TILE), BF16), vmem((D, Q_DEV), BF16),
                vmem((Q_DEV, D), BF16), vmem((D, D), BF16), pltpu.SemaphoreType.DMA((4,)),
            ],
        ),
        compiler_params=pltpu.CompilerParams(vmem_limit_bytes=VMEM_BYTES),
    )(lists, counts, order, kw, vw, q, dp, dpt, awt, qft, do, wq)


def grads_kernel(
    extents,
    pk_in, pv_in, w_in, wo_in, wk_in, wv_in,
    ag_out, wg_out,
    pk, pv, wk, wv,
    corner, passed, ends, end_s, end_r, side_s, side_r, corner_r, acc, ag_s, wg_s,
    mine, core_r, term, yf, yrl, ysum, xf, xrl, xsum,
    ta, tb, xa_r, yb_r, zs, zr,
    load_sem, store_sem, pass_send, pass_recv, end_send, end_recv, side_send, side_recv,
    cs_sem, cr_sem, ys_sem, yr_sem, xs_sem, xr_sem, xas_sem, xar_sem, ybs_sem, ybr_sem,
    zs_sem, zr_sem,
):
    gx, gy = lax.axis_index("gx"), lax.axis_index("gy")
    core = lax.rem(gy, 2)
    z = lax.rem(gx, 4) * 2 + gy // 2
    x = lax.rem(gx // 4, 4)
    y = gx // 16

    def device(y, x, z, core):
        return ((y * 4 + x) * 4 + z // 2, lax.rem(z, 2) * 2 + core)

    def exists(dx, dy):
        return inside((gx + dx, gy + dy), extents)

    groups = [slice(12, 16), slice(8, 12), slice(4, 8), slice(0, 4)]
    pairs = [(wk_in, wk), (wv_in, wv)]
    for at in groups:
        pairs += [(pk_in.at[:, at], pk.at[:, at]), (pv_in.at[:, at], pv.at[:, at])]
    def terms_in(m, half):
        if m < 3:
            return w_in.at[half, m]
        return wo_in.at[:, pl.ds(pl.multiple_of(half * HALF, 128), HALF)]

    pairs += [(terms_in(m, core), mine.at[m]) for m in range(4)]
    loads = [pltpu.make_async_copy(s, d, load_sem.at[i]) for i, (s, d) in enumerate(pairs)]
    for load in loads[0:4] + loads[10:14] + loads[4:10]:
        load.start()
    sibling = device(y, x, z, 1 - core)
    fixed = [sibling]
    fixed += [device(lax.rem(y + k, 4), x, z, core) for k in (1, 2, 3)]
    fixed += [device(y, lax.rem(x + k, 4), z, core) for k in (1, 2, 3)]
    fixed += [device(y, x, lax.rem(z + k, 8), c) for k in range(1, 8) for c in (0, 1)]
    greet([((gx + dx, gy + dy), exists(dx, dy)) for dx, dy in DIRS]
          + [(where, gx >= 0) for where in fixed])

    def remote(src, dst, send, recv, where):
        return pltpu.make_async_remote_copy(
            src_ref=src, dst_ref=dst, send_sem=send, recv_sem=recv,
            device_id=where, device_id_type=MESH,
        )

    def terms_of(group, goal):
        base = 4 * group

        def side(blocks):
            return jnp.concatenate(
                [blocks[h, base : base + 4].reshape(4 * TILE, TILE) for h in range(PAIRS)], axis=1
            )

        left_k, left_v = side(pk), side(pv)

        def step(j, _):
            at = pl.ds(pl.multiple_of(j * 256, 256), 256)
            part = nt(left_k, wk[at, :]) + nt(left_v, wv[at, :])
            for n in range(4):
                goal[n, :, at] = part[n * TILE : (n + 1) * TILE].astype(goal.dtype)
            return 0

        lax.fori_loop(0, 3, step, 0)

    def from_corner(rx, ry, direct):
        n, p = int(rx == 1), int(ry == 1)
        dst = corner_r.at[n] if direct else passed.at[n, 1 - p]
        return remote(corner.at[2 * p + n], dst, pass_send.at[n, p], pass_recv.at[n, 1 - p],
                      (gx + (rx if direct else 0), gy + ry))

    def from_end(rx, c):
        n = int(rx == 1)
        return remote(end_s.at[2 * n + c], end_r.at[n, c], end_send.at[n, c], end_recv.at[n, c],
                      (gx + rx, gy))

    def from_side(ry):
        p = int(ry == 1)
        return remote(side_s.at[2 * p : 2 * p + 2], side_r.at[p], side_send.at[p],
                      side_recv.at[p], (gx, gy + ry))

    need = {
        "C": (0, 1, 2, 3), "E": (0, 1, 4, 5), "S": (0, 1, 6, 7), "K": (0, 1, 8, 9),
        "A0": (10,), "A1": (11,), "A2": (12,), "A3": (13,),
    }

    def corner_terms():
        terms_of(3, corner)
        for rx, ry in ((-1, 1), (1, -1), (-1, -1), (1, 1)):
            direct = straight(-rx, -ry, gy + ry)

            @pl.when(exists(rx, ry) & direct)
            def _(rx=rx, ry=ry):
                from_corner(rx, ry, True).start()

            @pl.when(exists(rx, ry) & jnp.logical_not(direct))
            def _(rx=rx, ry=ry):
                from_corner(rx, ry, False).start()

    def send_ends():
        first = jnp.where(gy < 2, 0, 1)
        for turn in range(2):
            c = first if turn == 0 else 1 - first
            for rx in (-1, 1):
                n = int(rx == 1)
                waits = jnp.where(
                    c == 0,
                    exists(rx, -1) & jnp.logical_not(straight(-rx, -1, gy)),
                    exists(rx, 1) & jnp.logical_not(straight(-rx, 1, gy)),
                )

                @pl.when(exists(rx, 0) & waits)
                def _(rx=rx, n=n, c=c):
                    remote(corner.at[0], passed.at[n, c], pass_send.at[0, 0],
                           pass_recv.at[n, c], sibling).wait_recv()
                    end_s[2 * n + c] = (ends[2 * n + c] + passed[n, c].astype(F32)).astype(BF16)

                @pl.when(exists(rx, 0) & jnp.logical_not(waits))
                def _(n=n, c=c):
                    end_s[2 * n + c] = ends[2 * n + c].astype(BF16)

                @pl.when(exists(rx, 0))
                def _(rx=rx, c=c):
                    from_end(rx, c).start()

    def side_terms():
        terms_of(1, side_s)
        for ry in (-1, 1):
            @pl.when(exists(0, ry))
            def _(ry=ry):
                from_side(ry).start()

    def crossing(m):
        return remote(terms_in(m, 1 - core), core_r.at[m], cs_sem.at[m], cr_sem.at[m], sibling)

    y_up, y_down = device(lax.rem(y + 1, 4), x, z, core), device(lax.rem(y + 3, 4), x, z, core)
    x_next, x_over, x_last = lax.rem(x + 1, 4), lax.rem(x + 2, 4), lax.rem(x + 3, 4)
    x_up, x_down = device(y, x_next, z, core), device(y, x_last, z, core)

    def y_copy(m, i):
        low, high = slice(0, 2), slice(2, 4)
        src, dst, where = [
            (term.at[m, high, 0], yf.at[0, high], y_up),
            (term.at[m, low, 0], yf.at[1, low], y_down),
            (term.at[m, low, 0], yrl.at[0], y_up),
            (term.at[m, high, 0], yrl.at[1], y_down),
            (ysum.at[0], yf.at[0, low], y_up),
            (ysum.at[1], yf.at[1, high], y_down),
        ][i]
        return remote(src, dst, ys_sem.at[i], yr_sem.at[i], where)

    def x_copy(m, i):
        low, high = slice(0, 48), slice(48, 96)
        src, dst, where = [
            (term.at[m, x_next, 1, high], xf.at[m, 0, high], x_up),
            (term.at[m, x_last, 1, low], xf.at[m, 1, low], x_down),
            (term.at[m, x_over, 1, low], xrl.at[m, 0], x_up),
            (term.at[m, x_over, 1, high], xrl.at[m, 1], x_down),
            (xsum.at[m, 0], xf.at[m, 0, low], x_up),
            (xsum.at[m, 1], xf.at[m, 1, high], x_down),
        ][i]
        return remote(src, dst, xs_sem.at[m, i], xr_sem.at[m, i], where)

    def y_place(m):
        return lax.rem(m - y + 4, 4)

    def add_cores(m):
        crossing(m).wait()
        for goal in range(4):
            for part in range(2):
                at = slice(goal * 192 + part * 96, goal * 192 + part * 96 + 96)
                term[m, goal, part] = (
                    mine[m, at].astype(F32) + core_r[m, at].astype(F32)
                ).astype(BF16)

        @pl.when(y_place(m) == 2)
        def _():
            y_copy(m, 2).start()
            y_copy(m, 3).start()

        for i in (2, 3):
            x_copy(m, i).start()

    def send_next(m):
        @pl.when(y_place(m) == 1)
        def _():
            y_copy(m, 0).start()

        @pl.when(y_place(m) == 3)
        def _():
            y_copy(m, 1).start()

        for i in (0, 1):
            x_copy(m, i).start()

    def hand_on(m):
        @pl.when(y_place(m) == 1)
        def _():
            y_copy(m, 2).wait_recv()
            for goal in range(2):
                ysum[0, goal] = (
                    term[m, goal, 0].astype(F32) + yrl[0, goal].astype(F32)
                ).astype(BF16)
            y_copy(m, 4).start()

        @pl.when(y_place(m) == 3)
        def _():
            y_copy(m, 3).wait_recv()
            for goal in range(2):
                ysum[1, goal] = (
                    term[m, 2 + goal, 0].astype(F32) + yrl[1, goal].astype(F32)
                ).astype(BF16)
            y_copy(m, 5).start()

        for n, goal in ((0, x_next), (1, x_last)):
            x_copy(m, 2 + n).wait_recv()
            at = slice(48 * n, 48 * n + 48)
            xsum[m, n] = (
                term[m, goal, 1, at].astype(F32) + xrl[m, n].astype(F32)
            ).astype(BF16)
            x_copy(m, 4 + n).start()

    steps = {
        "C": corner_terms, "E": lambda: terms_of(2, ends), "G": send_ends, "S": side_terms,
        "K": lambda: terms_of(0, acc),
    }
    for m in range(4):
        steps["A%d" % m] = partial(add_cores, m)
        steps["B%d" % m] = partial(send_next, m)
        steps["H%d" % m] = partial(hand_on, m)
    def cross():
        for m in range(4):
            crossing(m).start()

    steps["X"] = cross
    loaded = set()
    for step in ORDER:
        for i in need.get(step, ()):
            if i not in loaded:
                loaded.add(i)
                loads[i].wait()
        steps[step]()

    for i in (0, 1, 4, 5):
        y_copy(0, i).wait_recv()
    for goal in range(4):
        total = term[y, goal, 0].astype(F32)
        ta[goal] = (total + yf[0, goal].astype(F32) + yf[1, goal].astype(F32)).astype(BF16)

    def to_column_second(k):
        goal = lax.rem(x + k, 4)
        return remote(ta.at[goal], xa_r.at[3 - k], xas_sem.at[k - 1], xar_sem.at[3 - k],
                      device(y, goal, z, core))

    for k in (2, 1, 3):
        to_column_second(k).start()
    for m in range(4):
        for i in (0, 1, 4, 5):
            x_copy(m, i).wait_recv()
        total = term[m, x, 1].astype(F32)
        tb[m] = (total + xf[m, 0].astype(F32) + xf[m, 1].astype(F32)).astype(BF16)

    def to_row_second(k):
        goal = lax.rem(y + k, 4)
        return remote(tb.at[goal], yb_r.at[3 - k], ybs_sem.at[k - 1], ybr_sem.at[3 - k],
                      device(goal, x, z, core))

    for k in (2, 1, 3):
        to_row_second(k).start()

    zs[...] = jnp.zeros((8, 2, 16, HALF), BF16)

    def cut(total, base):
        for i in range(4):
            for c in range(2):
                row = i * 24 + c * 12
                zs[base + i, c, 0:12] = total[row : row + 12].astype(BF16)

    for k in (1, 2, 3):
        to_column_second(k).wait_recv()
    total = ta[x].astype(F32)
    for slot in range(3):
        total = total + xa_r[slot].astype(F32)
    cut(total, 0)
    for k in (1, 2, 3):
        to_row_second(k).wait_recv()
    total = tb[y].astype(F32)
    for slot in range(3):
        total = total + yb_r[slot].astype(F32)
    cut(total, 4)

    def along(k, c):
        goal = lax.rem(z + k, 8)
        return remote(zs.at[goal, c], zr.at[core, 7 - k], zs_sem.at[k, c], zr_sem.at[core, 7 - k],
                      device(y, x, goal, c))

    def across():
        return remote(zs.at[z, 1 - core], zr.at[core, 7], zs_sem.at[0, 0], zr_sem.at[core, 7],
                      sibling)

    for k in (4, 3, 5, 2, 6, 1, 7):
        for c in (0, 1):
            along(k, c).start()
    across().start()

    for ry in (-1, 1):
        @pl.when(exists(0, -ry))
        def _(ry=ry):
            from_side(ry).wait_recv()
            p, c = (1, 0) if ry == 1 else (0, 1)
            for r in range(2):
                acc[2 * r + c] += side_r[p, r].astype(F32)
    for rx in (-1, 1):
        n, r = (1, 0) if rx == 1 else (0, 1)

        @pl.when(exists(-rx, 0))
        def _(rx=rx, n=n, r=r):
            for c in range(2):
                from_end(rx, c).wait_recv()
                acc[2 * r + c] += end_r[n, c].astype(F32)
    for rx, ry in ((-1, 1), (1, -1)):
        n, r = (1, 0) if rx == 1 else (0, 1)
        p, c = (1, 0) if ry == 1 else (0, 1)

        @pl.when(exists(-rx, -ry) & straight(-rx, -ry, gy))
        def _(rx=rx, ry=ry, n=n, p=p, r=r, c=c):
            remote(corner.at[0], corner_r.at[n], pass_send.at[0, 0], pass_recv.at[n, 1 - p],
                   sibling).wait_recv()
            acc[2 * r + c] += corner_r[n].astype(F32)

    ag_s[...] = acc[...].astype(BF16)
    ag_copy = pltpu.make_async_copy(ag_s, ag_out, store_sem.at[0])
    ag_copy.start()

    def arrived(c, slot):
        remote(zs.at[0, 0], zr.at[c, slot], zs_sem.at[0, 0], zr_sem.at[c, slot],
               sibling).wait_recv()
        return zr[c, slot].astype(F32)

    held = zs[z, core].astype(F32)
    for slot in range(7):
        held = held + arrived(core, slot)
    other = arrived(1 - core, 7)
    for slot in range(7):
        other = other + arrived(1 - core, slot)
    low = core == 0
    held, other = held[0:12], other[0:12]
    norm = (extents[0] * extents[1] * Q_DEV) ** (-0.5)
    wg_s[:, 0:HALF] = jnp.where(low, held, other) * norm
    wg_s[:, HALF:D] = jnp.where(low, other, held) * norm
    wg_copy = pltpu.make_async_copy(wg_s, wg_out, store_sem.at[1])
    wg_copy.start()

    for rx in (-1, 1):
        @pl.when(exists(rx, 0))
        def _(rx=rx):
            from_end(rx, 0).wait_send()
            from_end(rx, 1).wait_send()
        for ry in (-1, 1):
            @pl.when(exists(rx, ry))
            def _(rx=rx, ry=ry):
                from_corner(rx, ry, False).wait_send()
    for ry in (-1, 1):
        @pl.when(exists(0, ry))
        def _(ry=ry):
            from_side(ry).wait_send()
    for i in range(6):
        y_copy(0, i).wait_send()
    for m in range(4):
        for i in range(6):
            x_copy(m, i).wait_send()
    for k in (1, 2, 3):
        to_column_second(k).wait_send()
        to_row_second(k).wait_send()
    for k in range(1, 8):
        for c in (0, 1):
            along(k, c).wait_send()
    across().wait_send()
    ag_copy.wait()
    wg_copy.wait()


def grads(extents, pk, pv, w, wo, wk, wv):
    any_spec = pl.BlockSpec(memory_space=pl.ANY)
    blocks = (PAIRS, 16, TILE, TILE)
    square = (D, D)
    four, two = (4, TILE, D), (2, 2, TILE, D)
    dma = pltpu.SemaphoreType.DMA
    held = [
        (blocks, BF16), (blocks, BF16), (square, BF16), (square, BF16),
        (four, BF16), (two, BF16), (four, F32), (four, BF16), (two, BF16), (four, BF16),
        (two, BF16), ((2, TILE, D), BF16), (four, F32), (four, BF16),
        ((12, D), F32),
        ((4, D, HALF), BF16), ((4, D, HALF), BF16),
        ((4, 4, 2, 96, HALF), BF16),
        ((2, 4, 96, HALF), BF16), ((2, 2, 96, HALF), BF16), ((2, 2, 96, HALF), BF16),
        ((4, 2, 96, HALF), BF16), ((4, 2, 48, HALF), BF16), ((4, 2, 48, HALF), BF16),
        ((4, 96, HALF), BF16), ((4, 96, HALF), BF16), ((3, 96, HALF), BF16),
        ((3, 96, HALF), BF16), ((8, 2, 16, HALF), BF16), ((2, 8, 16, HALF), BF16),
    ]
    sems = [(14,), (2,), (2, 2), (2, 2), (2, 2), (2, 2), (2,), (2,), (4,), (4,), (6,), (6,),
            (4, 6), (4, 6), (3,), (3,), (3,), (3,), (8, 2), (2, 8)]
    anchor_grad, weight_grads = pl.pallas_call(
        partial(grads_kernel, extents),
        name="grads",
        out_shape=[
            jax.ShapeDtypeStruct(four, BF16),
            jax.ShapeDtypeStruct((12, D), F32),
        ],
        in_specs=[any_spec] * 6,
        out_specs=[any_spec] * 2,
        scratch_shapes=[pltpu.VMEM(s, t) for s, t in held] + [dma(s) for s in sems],
        compiler_params=pltpu.CompilerParams(
            collective_id=1, has_side_effects=True, vmem_limit_bytes=VMEM_BYTES
        ),
    )(pk, pv, w, wo, wk, wv)
    return anchor_grad, weight_grads


def settle_kernel(ag_in, wg_in, ag_out, wg_out, ag, wg, sem):
    loads = [
        pltpu.make_async_copy(ag_in.at[n], ag.at[n], sem.at[0, n]) for n in range(4)
    ] + [pltpu.make_async_copy(wg_in, wg, sem.at[0, 4])]
    stores = [
        pltpu.make_async_copy(ag.at[n], ag_out.at[n], sem.at[1, n]) for n in range(4)
    ] + [pltpu.make_async_copy(wg, wg_out, sem.at[1, 4])]
    for load in loads:
        load.start()
    for load, store in zip(loads, stores):
        load.wait()
        store.start()
    for store in stores:
        store.wait()


def settle(anchor_grad, weight_grads):
    any_spec = pl.BlockSpec(memory_space=pl.ANY)
    held = (anchor_grad, weight_grads)
    return pl.pallas_call(
        settle_kernel,
        name="settle",
        out_shape=[jax.ShapeDtypeStruct(h.shape, h.dtype) for h in held],
        in_specs=[any_spec] * 2,
        out_specs=[any_spec] * 2,
        scratch_shapes=[pltpu.VMEM(h.shape, h.dtype) for h in held]
        + [pltpu.SemaphoreType.DMA((2, 5))],
        compiler_params=pltpu.CompilerParams(vmem_limit_bytes=VMEM_BYTES),
    )(*held)


def on_device(
    extents,
    query_feats, anchors, tile_lists, tile_counts, out_grad, w_query, w_key, w_value, w_out,
):
    qf = query_feats.reshape(Q_DEV, D)
    do = out_grad.reshape(Q_DEV, D)
    order = jnp.array([HELD.index((w // 4, w % 4)) for w in range(16)], jnp.int32)
    kw, vw, awt, q, dp, dpt, qft = halo(extents, anchors, qf, do, w_query, w_key, w_value, w_out)
    pk, pv, w, wo, query_grad = attention(
        tile_lists, tile_counts, order, kw, vw, q, dp, dpt, awt, qft, do, w_query
    )
    anchor_grad, weight_grads = settle(*grads(extents, pk, pv, w, wo, w_key, w_value))
    return query_grad.reshape(query_feats.shape), anchor_grad.reshape(anchors.shape), weight_grads


def solution(mesh):
    four = P("gx", "gy", None, None)
    in_specs = (four, four, four, P("gx", "gy", None), four, P(), P(), P(), P())
    out_specs = (four, four, P(("gx", "gy"), None))
    extents = (mesh.shape["gx"], mesh.shape["gy"])
    return jax.shard_map(
        partial(on_device, extents),
        mesh=mesh, in_specs=in_specs, out_specs=out_specs, check_vma=False,
    )
```

```python
from functools import partial

import jax
import jax.numpy as jnp
from jax import lax
from jax.experimental import pallas as pl
from jax.experimental.pallas import tpu as pltpu
from jax.sharding import PartitionSpec as P

HEADS = 12
HEAD_DIM = 64
KT = 4
D = 768
TILE = 128
PAIRS = 6
Q_DEV = 512
SCALE = HEAD_DIM ** (-0.5)
HALF = 384
LOG2E = 1.4426950408889634
DEAD = 1e30
ORDER = (
    "X", "C", "A0", "B0", "A1", "B1", "S", "A2", "B2", "A3", "B3", "E", "G", "H0", "H1", "H2", "H3",
    "Y", "L0", "L1", "L2", "L3", "K", "Z",
)
MESH = pl.DeviceIdType.MESH
F32 = jnp.float32
BF16 = jnp.bfloat16
PIECES = ("q", "0", "1", "2", "o", "")
VMEM_BYTES = 56 * 1024 * 1024

DIRS = ((-1, 0), (1, 0), (-1, -1), (-1, 1), (1, -1), (1, 1), (0, -1), (0, 1))
CENTRE = ((1, 1), (1, 2), (2, 1), (2, 2))
BESIDE = ((1, 0), (2, 0), (1, 3), (2, 3))
ENDS = ((0, 1), (0, 2), (3, 1), (3, 2))
CORNERS = ((0, 0), (3, 0), (0, 3), (3, 3))
HELD = CENTRE + BESIDE + ENDS + CORNERS


def nn(left, right):
    return lax.dot_general(left, right, (((1,), (0,)), ((), ())), preferred_element_type=F32)


def nt(left, right):
    return lax.dot_general(left, right, (((1,), (1,)), ((), ())), preferred_element_type=F32)


def tn(left, right):
    return lax.dot_general(left, right, (((0,), (0,)), ((), ())), preferred_element_type=F32)


def inside(place, extents):
    (px, py), (nx, ny) = place, extents
    return (px >= 0) & (px < nx) & (py >= 0) & (py < ny)


def greet(partners):
    barrier = pltpu.get_barrier_semaphore()
    total = jnp.int32(0)
    for where, present in partners:
        @pl.when(present)
        def _():
            pl.semaphore_signal(barrier, inc=1, device_id=where, device_id_type=MESH)
        total = total + jnp.where(present, 1, 0).astype(jnp.int32)
    pl.semaphore_wait(barrier, total)


def straight(dx, dy, gy):
    return ((dx, dy) == (1, -1)) & (gy == 2) | ((dx, dy) == (-1, 1)) & (gy == 1)


def halo_kernel(
    extents,
    anchors, qf_in, do_in, wq_in, wk_in, wv_in, wo_in,
    kw_out, vw_out, awt_out, q_out, dp_out, dpt_out, qft_out,
    win, kw, vw, awt, qf, do, wq, wk, wv, wo, q_s, dp_s, dpt_s, qft_s,
    end_send, end_recv, side_send, side_recv, corner_send, corner_recv, load_sem, store_sem,
):
    gx, gy = lax.axis_index("gx"), lax.axis_index("gy")
    loads = [
        pltpu.make_async_copy(src, dst, load_sem.at[i])
        for i, (src, dst) in enumerate(
            [(qf_in, qf), (wq_in, wq), (do_in, do), (wo_in, wo), (wk_in, wk), (wv_in, wv)]
        )
    ]
    own = pltpu.make_async_copy(anchors, win.at[1:3, 1:3], load_sem.at[6])
    for load in loads:
        load.start()
    own.start()
    greet([((gx + dx, gy + dy), inside((gx + dx, gy + dy), extents)) for dx, dy in DIRS])

    def exists(dx, dy):
        return inside((gx + dx, gy + dy), extents)

    def remote(src, dst, send, recv, dx, dy):
        return pltpu.make_async_remote_copy(
            src_ref=src, dst_ref=dst, send_sem=send, recv_sem=recv,
            device_id=(gx + dx, gy + dy), device_id_type=MESH,
        )

    def to_end(dx, c):
        n, row, goal = (0, 1, 0) if dx == 1 else (1, 0, 3)
        return remote(anchors.at[row, c], win.at[goal, c + 1], end_send.at[n, c],
                      end_recv.at[n, c], dx, 0)

    def to_side(dy):
        n, col, goal = (0, 1, 0) if dy == 1 else (1, 0, 3)
        return remote(anchors.at[:, col], win.at[1:3, goal], side_send.at[n], side_recv.at[n],
                      0, dy)

    def to_corner(dx, dy, direct):
        row, goal_row = (1, 0) if dx == 1 else (0, 3)
        col, goal_col = (1, 0) if dy == 1 else (0, 3)
        n, p = int(dx == -1), int(dy == -1)
        src = anchors.at[row, col] if direct else win.at[goal_row, col + 1]
        return remote(src, win.at[goal_row, goal_col], corner_send.at[n, p],
                      corner_recv.at[n, p], dx if direct else 0, dy)

    first = jnp.where(gy < 2, 1, 0)
    for turn in range(2):
        for dx in (1, -1):
            @pl.when(exists(dx, 0))
            def _(turn=turn, dx=dx):
                to_end(dx, first if turn == 0 else 1 - first).start()
    for dx, dy in ((1, -1), (-1, 1)):
        @pl.when(exists(dx, dy) & straight(dx, dy, gy))
        def _(dx=dx, dy=dy):
            to_corner(dx, dy, True).start()
    for dy in (1, -1):
        @pl.when(exists(0, dy))
        def _(dy=dy):
            to_side(dy).start()

    for dx, dy in DIRS:
        p0, p1 = {-1: (3, 4), 0: (1, 3), 1: (0, 1)}[dx]
        q0, q1 = {-1: (3, 4), 0: (1, 3), 1: (0, 1)}[dy]

        @pl.when(jnp.logical_not(exists(-dx, -dy)))
        def _(p0=p0, p1=p1, q0=q0, q1=q1):
            win[p0:p1, q0:q1] = jnp.zeros((p1 - p0, q1 - q0, TILE, D), BF16)

    loads[0].wait()
    loads[1].wait()

    def project_query(j, _):
        at = pl.ds(pl.multiple_of(j * 256, 256), 256)
        q_s[:, at] = (nn(qf[...], wq[:, at]).astype(BF16) * SCALE).astype(BF16)
        return 0

    lax.fori_loop(0, 3, project_query, 0)
    loads[2].wait()
    loads[3].wait()

    def project_dout(j, _):
        at = pl.ds(pl.multiple_of(j * 256, 256), 256)
        dp_s[:, at] = nt(do[...], wo[at, :]).astype(BF16)
        dpt_s[at, :] = nt(wo[at, :], do[...]).astype(BF16)
        qft_s[at, :] = qf[:, at].T
        return 0

    lax.fori_loop(0, 3, project_dout, 0)
    stores = []

    def store(src, dst):
        copy = pltpu.make_async_copy(src, dst, store_sem.at[len(stores)])
        copy.start()
        stores.append(copy)

    store(q_s, q_out)
    store(dp_s, dp_out)
    store(dpt_s, dpt_out)
    store(qft_s, qft_out)
    loads[4].wait()
    loads[5].wait()
    own.wait()

    def project_tiles(places, base):
        rows = jnp.concatenate([win[r, c] for r, c in places], axis=0)
        count = len(places)

        def step(j, _):
            at = pl.ds(pl.multiple_of(j * 256, 256), 256)
            for weight, goal in ((wk, kw), (wv, vw)):
                part = nn(rows, weight[:, at]).astype(BF16)
                for n in range(count):
                    for i in range(2):
                        goal[2 * j + i, base + n] = part[
                            n * TILE : (n + 1) * TILE, i * TILE : (i + 1) * TILE
                        ]
            return 0

        lax.fori_loop(0, 3, step, 0, unroll=True)
        for n, (r, c) in enumerate(places):
            awt[:, pl.ds(pl.multiple_of((base + n) * TILE, TILE), TILE)] = win[r, c].T
        at = pl.ds(base, count)
        wide = pl.ds(pl.multiple_of(base * TILE, TILE), count * TILE)
        store(kw.at[:, at], kw_out.at[:, at])
        store(vw.at[:, at], vw_out.at[:, at])
        store(awt.at[:, wide], awt_out.at[:, wide])

    project_tiles(CENTRE, 0)
    for dy in (1, -1):
        @pl.when(exists(0, -dy))
        def _(dy=dy):
            to_side(dy).wait_recv()
    project_tiles(BESIDE, 4)
    for turn in range(2):
        for dx in (1, -1):
            c = first if turn == 0 else 1 - first

            @pl.when(exists(-dx, 0))
            def _(dx=dx, c=c):
                to_end(dx, c).wait_recv()

            for dy, col in ((1, 1), (-1, 0)):
                @pl.when(exists(-dx, 0) & exists(0, dy) & (c == col)
                         & jnp.logical_not(straight(dx, dy, gy)))
                def _(dx=dx, dy=dy):
                    to_corner(dx, dy, False).start()
    project_tiles(ENDS, 8)
    for turn in range(2):
        side = lax.rem(gy + 1 + turn, 2)
        for dy, p in ((1, 0), (-1, 1)):
            for dx in (1, -1):
                @pl.when(exists(-dx, -dy) & (side == p))
                def _(dx=dx, dy=dy):
                    to_corner(dx, dy, True).wait_recv()
        project_tiles([(0, 3 * side), (3, 3 * side)], 12 + 2 * side)
    for dx in (1, -1):
        @pl.when(exists(dx, 0))
        def _(dx=dx):
            to_end(dx, 0).wait_send()
            to_end(dx, 1).wait_send()
        for dy in (1, -1):
            here = straight(dx, dy, gy)

            @pl.when(exists(dx, dy) & here | exists(-dx, dy) & jnp.logical_not(here))
            def _(dx=dx, dy=dy):
                to_corner(dx, dy, True).wait_send()
    for dy in (1, -1):
        @pl.when(exists(0, dy))
        def _(dy=dy):
            to_side(dy).wait_send()
    for copy in stores:
        copy.wait()


def halo(extents, anchors, qf, do, wq, wk, wv, wo):
    any_spec = pl.BlockSpec(memory_space=pl.ANY)
    blocks = (PAIRS, 16, TILE, TILE)
    tall, wide = (Q_DEV, D), (D, Q_DEV)
    square = (D, D)
    shapes = [blocks, blocks, (D, 16 * TILE), tall, tall, wide, wide]
    return pl.pallas_call(
        partial(halo_kernel, extents),
        name="halo",
        out_shape=[jax.ShapeDtypeStruct(s, BF16) for s in shapes],
        in_specs=[any_spec] * 7,
        out_specs=[any_spec] * 7,
        scratch_shapes=[
            pltpu.VMEM(s, BF16)
            for s in [(4, 4, TILE, D), blocks, blocks, (D, 16 * TILE), tall, tall,
                      square, square, square, square, tall, tall, wide, wide]
        ]
        + [
            pltpu.SemaphoreType.DMA(s)
            for s in [(2, 2), (2, 2), (2,), (2,), (2, 2), (2, 2), (7,), (19,)]
        ],
        compiler_params=pltpu.CompilerParams(
            collective_id=0, has_side_effects=True, vmem_limit_bytes=VMEM_BYTES
        ),
    )(anchors, qf, do, wq, wk, wv, wo)


def attention_kernel(
    lists, counts, order, kw, vw, q_ref, dp_ref, dpt_ref, awt_in, qft_in, do_in, wq_in,
    pk_out, pv_out, w_out, wo_out, qg_out,
    dk, dv, kv, att_s, dq_s, awt, qft, do_s, wq, sem,
):
    pair = pl.program_id(0)
    loads = [
        pltpu.make_async_copy(src, dst, sem.at[i])
        for i, (src, dst) in enumerate([(qft_in, qft), (do_in, do_s), (awt_in, awt), (wq_in, wq)])
    ]

    @pl.when(pair == 0)
    def _():
        for load in loads:
            load.start()

    slot, last = lax.rem(pair, 2), lax.rem(pair + 1, 2)

    def kept(which):
        return pl.ds(pl.multiple_of(which * TILE, TILE), TILE)

    before = kept(jnp.maximum(pair - 1, 0))

    def pair_weights(i):
        at = slice(i * 256, (i + 1) * 256)
        both = nn(awt[at, :], kv[last]).astype(BF16)
        w_out[0, 1, at, :] = both[:, :TILE]
        w_out[0, 2, at, :] = both[:, TILE:]

    def query_weights():
        w_out[0, 0] = nn(qft[...], dq_s[:, before]).astype(BF16)

    def out_weights():
        wo_out[...] = nn(att_s[last], do_s[...]).astype(BF16)

    first = lax.broadcasted_iota(jnp.int32, (TILE, TILE), 1) < HEAD_DIM

    def products(b):
        tiles = [order[lists[0, 0, b, s]] for s in range(KT)]
        at = slice(b * TILE, (b + 1) * TILE)
        q, do = q_ref[at, :], dp_ref[at, :]
        zero = jnp.zeros_like(q)
        q2 = jnp.concatenate([jnp.where(first, q, zero), jnp.where(first, zero, q)], axis=0)
        do2 = jnp.concatenate([jnp.where(first, do, zero), jnp.where(first, zero, do)], axis=0)
        keys = jnp.concatenate([kw[0, t] for t in tiles], axis=0)
        values = jnp.concatenate([vw[0, t] for t in tiles], axis=0)
        return b, at, tiles, q2, do2, keys, values, nt(keys, q2), nt(values, do2)

    def softmax(state):
        b, at, tiles, q2, do2, keys, values, scores, dprob = state
        live = [s < counts[0, 0, b] for s in range(KT)]
        slots = [scores[s * TILE : (s + 1) * TILE] for s in range(KT)]
        top = jnp.max(slots[0], axis=0, keepdims=True)
        for s in range(1, KT):
            best = jnp.max(slots[s], axis=0, keepdims=True)
            top = jnp.maximum(top, jnp.where(live[s], best, -jnp.inf))
        top = top * LOG2E
        expo = jnp.concatenate(
            [
                jnp.exp2(slots[s] * LOG2E - (top + jnp.where(live[s], 0.0, DEAD).astype(F32)))
                for s in range(KT)
            ],
            axis=0,
        )
        prob = expo * (1.0 / jnp.sum(expo, axis=0, keepdims=True))
        half = prob.astype(BF16)
        att2 = tn(values, half)
        att = jnp.concatenate(
            [att2[:HEAD_DIM, :TILE], att2[HEAD_DIM:, TILE:]], axis=0
        ).astype(BF16)
        att_s[slot, :, at] = att
        both = att.astype(F32) * dpt_ref[:, at].astype(F32)
        delta = jnp.concatenate(
            [
                jnp.sum(both[:HEAD_DIM], axis=0, keepdims=True),
                jnp.sum(both[HEAD_DIM:], axis=0, keepdims=True),
            ],
            axis=1,
        )
        return at, tiles, q2, do2, keys, half, (prob * (dprob - delta)).astype(BF16)

    def gradients(state):
        at, tiles, q2, do2, keys, half, dscore = state
        dq2 = tn(keys, dscore)
        dq = jnp.concatenate([dq2[:HEAD_DIM, :TILE], dq2[HEAD_DIM:, TILE:]], axis=0) * SCALE
        dq_s[at, kept(pair)] = dq.T.astype(BF16)
        dkey = nn(dscore, q2)
        dvalue = nn(half, do2)
        for s in range(KT):
            dk[tiles[s]] += dkey[s * TILE : (s + 1) * TILE]
            dv[tiles[s]] += dvalue[s * TILE : (s + 1) * TILE]

    def all_blocks(weights):
        dk[...] = jnp.zeros_like(dk)
        dv[...] = jnp.zeros_like(dv)
        ahead, behind = {}, {}
        for turn in range(6):
            if turn < 4:
                ahead[turn] = products(turn)
            if 1 <= turn < 5:
                behind[turn - 1] = softmax(ahead.pop(turn - 1))
            if weights:
                for piece in PIECES[turn].split():
                    if piece == "q":
                        query_weights()
                    elif piece == "o":
                        out_weights()
                    else:
                        pair_weights(int(piece))
            if turn >= 2:
                gradients(behind.pop(turn - 2))
        for t in range(16):
            key_part, value_part = dk[t].astype(BF16), dv[t].astype(BF16)
            pk_out[0, t] = key_part
            pv_out[0, t] = value_part
            kv[slot, t * TILE : (t + 1) * TILE, :TILE] = key_part
            kv[slot, t * TILE : (t + 1) * TILE, TILE:] = value_part

    @pl.when(pair == 0)
    def _():
        all_blocks(False)
        for load in loads:
            load.wait()

    @pl.when((pair > 0) & (pair < PAIRS))
    def _():
        all_blocks(True)

    @pl.when(pair == PAIRS)
    def _():
        out_weights()
        query_weights()
        for i in range(3):
            pair_weights(i)
        for i in range(3):
            at = slice(i * 256, (i + 1) * 256)
            qg_out[:, at] = nt(dq_s[...], wq[at, :]).astype(BF16)


def attention(lists, counts, order, kw, vw, q, dp, dpt, awt, qft, do, wq):
    blocks = (PAIRS, 16, TILE, TILE)
    here = lambda p: jnp.minimum(p, PAIRS - 1)
    past = lambda p: jnp.maximum(p - 1, 0)
    by_pair = pl.BlockSpec((1, 16, TILE, TILE), lambda p, *_: (here(p), 0, 0, 0))
    tall = pl.BlockSpec((Q_DEV, TILE), lambda p, *_: (0, here(p)))
    wide = pl.BlockSpec((TILE, Q_DEV), lambda p, *_: (here(p), 0))
    any_spec = pl.BlockSpec(memory_space=pl.ANY)
    vmem = pltpu.VMEM
    return pl.pallas_call(
        attention_kernel,
        name="attention",
        out_shape=[
            jax.ShapeDtypeStruct(blocks, BF16),
            jax.ShapeDtypeStruct(blocks, BF16),
            jax.ShapeDtypeStruct((2, 3, D, HALF), BF16),
            jax.ShapeDtypeStruct((D, D), BF16),
            jax.ShapeDtypeStruct((Q_DEV, D), BF16),
        ],
        grid_spec=pltpu.PrefetchScalarGridSpec(
            num_scalar_prefetch=3,
            grid=(PAIRS + 1,),
            in_specs=[by_pair, by_pair, tall, tall, wide] + [any_spec] * 4,
            out_specs=[
                by_pair,
                by_pair,
                pl.BlockSpec((1, 3, D, TILE), lambda p, *_: (past(p) // 3, 0, 0, past(p) % 3)),
                pl.BlockSpec((TILE, D), lambda p, *_: (past(p), 0)),
                pl.BlockSpec((Q_DEV, D), lambda p, *_: (0, 0)),
            ],
            scratch_shapes=[
                vmem((16, TILE, TILE), F32), vmem((16, TILE, TILE), F32),
                vmem((2, 16 * TILE, 2 * TILE), BF16), vmem((2, TILE, Q_DEV), BF16),
                vmem((Q_DEV, D), BF16), vmem((D, 16 * TILE), BF16), vmem((D, Q_DEV), BF16),
                vmem((Q_DEV, D), BF16), vmem((D, D), BF16), pltpu.SemaphoreType.DMA((4,)),
            ],
        ),
        compiler_params=pltpu.CompilerParams(vmem_limit_bytes=VMEM_BYTES),
    )(lists, counts, order, kw, vw, q, dp, dpt, awt, qft, do, wq)


def grads_kernel(
    extents,
    pk_in, pv_in, w_in, wo_in, wk_in, wv_in,
    ag_out, wg_out,
    pk, pv, wk, wv,
    corner, passed, ends, end_s, end_r, side_s, side_r, corner_r, acc, ag_s, wg_s,
    mine, core_r, term, yf, yrl, ysum, xf, xrl, xsum,
    ta, tb, xa_r, yb_r, zs, zr,
    load_sem, store_sem, pass_send, pass_recv, end_send, end_recv, side_send, side_recv,
    cs_sem, cr_sem, ys_sem, yr_sem, xs_sem, xr_sem, xas_sem, xar_sem, ybs_sem, ybr_sem,
    zs_sem, zr_sem,
):
    gx, gy = lax.axis_index("gx"), lax.axis_index("gy")
    core = lax.rem(gy, 2)
    z = lax.rem(gx, 4) * 2 + gy // 2
    x = lax.rem(gx // 4, 4)
    y = gx // 16

    def device(y, x, z, core):
        return ((y * 4 + x) * 4 + z // 2, lax.rem(z, 2) * 2 + core)

    def exists(dx, dy):
        return inside((gx + dx, gy + dy), extents)

    groups = [slice(12, 16), slice(8, 12), slice(4, 8), slice(0, 4)]
    pairs = [(wk_in, wk), (wv_in, wv)]
    for at in groups:
        pairs += [(pk_in.at[:, at], pk.at[:, at]), (pv_in.at[:, at], pv.at[:, at])]
    def terms_in(m, half):
        if m < 3:
            return w_in.at[half, m]
        return wo_in.at[:, pl.ds(pl.multiple_of(half * HALF, 128), HALF)]

    pairs += [(terms_in(m, core), mine.at[m]) for m in range(4)]
    loads = [pltpu.make_async_copy(s, d, load_sem.at[i]) for i, (s, d) in enumerate(pairs)]
    for load in loads[0:4] + loads[6:8] + loads[10:14] + loads[4:6] + loads[8:10]:
        load.start()
    sibling = device(y, x, z, 1 - core)
    fixed = [sibling]
    fixed += [device(lax.rem(y + k, 4), x, z, core) for k in (1, 2, 3)]
    fixed += [device(y, lax.rem(x + k, 4), z, core) for k in (1, 2, 3)]
    fixed += [device(y, x, lax.rem(z + k, 8), c) for k in range(1, 8) for c in (0, 1)]
    greet([((gx + dx, gy + dy), exists(dx, dy)) for dx, dy in DIRS]
          + [(where, gx >= 0) for where in fixed])

    def remote(src, dst, send, recv, where):
        return pltpu.make_async_remote_copy(
            src_ref=src, dst_ref=dst, send_sem=send, recv_sem=recv,
            device_id=where, device_id_type=MESH,
        )

    def terms_of(group, goal):
        base = 4 * group

        def side(blocks):
            return jnp.concatenate(
                [blocks[h, base : base + 4].reshape(4 * TILE, TILE) for h in range(PAIRS)], axis=1
            )

        left_k, left_v = side(pk), side(pv)

        def step(j, _):
            at = pl.ds(pl.multiple_of(j * 256, 256), 256)
            part = nt(left_k, wk[at, :]) + nt(left_v, wv[at, :])
            for n in range(4):
                goal[n, :, at] = part[n * TILE : (n + 1) * TILE].astype(goal.dtype)
            return 0

        lax.fori_loop(0, 3, step, 0)

    def from_corner(rx, ry, direct):
        n, p = int(rx == 1), int(ry == 1)
        dst = corner_r.at[n] if direct else passed.at[n, 1 - p]
        return remote(corner.at[2 * p + n], dst, pass_send.at[n, p], pass_recv.at[n, 1 - p],
                      (gx + (rx if direct else 0), gy + ry))

    def from_end(rx, c):
        n = int(rx == 1)
        return remote(end_s.at[2 * n + c], end_r.at[n, c], end_send.at[n, c], end_recv.at[n, c],
                      (gx + rx, gy))

    def from_side(ry):
        p = int(ry == 1)
        return remote(side_s.at[2 * p : 2 * p + 2], side_r.at[p], side_send.at[p],
                      side_recv.at[p], (gx, gy + ry))

    need = {
        "C": (0, 1, 2, 3), "E": (0, 1, 4, 5), "S": (0, 1, 6, 7), "K": (0, 1, 8, 9),
        "A0": (10,), "A1": (11,), "A2": (12,), "A3": (13,),
    }

    def corner_terms():
        terms_of(3, corner)
        for rx, ry in ((-1, 1), (1, -1), (-1, -1), (1, 1)):
            direct = straight(-rx, -ry, gy + ry)

            @pl.when(exists(rx, ry) & direct)
            def _(rx=rx, ry=ry):
                from_corner(rx, ry, True).start()

            @pl.when(exists(rx, ry) & jnp.logical_not(direct))
            def _(rx=rx, ry=ry):
                from_corner(rx, ry, False).start()

    def send_ends():
        first = jnp.where(gy < 2, 0, 1)
        for turn in range(2):
            c = first if turn == 0 else 1 - first
            for rx in (-1, 1):
                n = int(rx == 1)
                waits = jnp.where(
                    c == 0,
                    exists(rx, -1) & jnp.logical_not(straight(-rx, -1, gy)),
                    exists(rx, 1) & jnp.logical_not(straight(-rx, 1, gy)),
                )

                @pl.when(exists(rx, 0) & waits)
                def _(rx=rx, n=n, c=c):
                    remote(corner.at[0], passed.at[n, c], pass_send.at[0, 0],
                           pass_recv.at[n, c], sibling).wait_recv()
                    end_s[2 * n + c] = (ends[2 * n + c] + passed[n, c].astype(F32)).astype(BF16)

                @pl.when(exists(rx, 0) & jnp.logical_not(waits))
                def _(n=n, c=c):
                    end_s[2 * n + c] = ends[2 * n + c].astype(BF16)

                @pl.when(exists(rx, 0))
                def _(rx=rx, c=c):
                    from_end(rx, c).start()

    def side_terms():
        terms_of(1, side_s)
        for ry in (-1, 1):
            @pl.when(exists(0, ry))
            def _(ry=ry):
                from_side(ry).start()

    def crossing(m):
        return remote(terms_in(m, 1 - core), core_r.at[m], cs_sem.at[m], cr_sem.at[m], sibling)

    y_up, y_down = device(lax.rem(y + 1, 4), x, z, core), device(lax.rem(y + 3, 4), x, z, core)
    x_next, x_over, x_last = lax.rem(x + 1, 4), lax.rem(x + 2, 4), lax.rem(x + 3, 4)
    x_up, x_down = device(y, x_next, z, core), device(y, x_last, z, core)

    def y_copy(m, i):
        low, high = slice(0, 2), slice(2, 4)
        src, dst, where = [
            (term.at[m, high, 0], yf.at[0, high], y_up),
            (term.at[m, low, 0], yf.at[1, low], y_down),
            (term.at[m, low, 0], yrl.at[0], y_up),
            (term.at[m, high, 0], yrl.at[1], y_down),
            (ysum.at[0], yf.at[0, low], y_up),
            (ysum.at[1], yf.at[1, high], y_down),
        ][i]
        return remote(src, dst, ys_sem.at[i], yr_sem.at[i], where)

    def x_copy(m, i):
        low, high = slice(0, 48), slice(48, 96)
        src, dst, where = [
            (term.at[m, x_next, 1, high], xf.at[m, 0, high], x_up),
            (term.at[m, x_last, 1, low], xf.at[m, 1, low], x_down),
            (term.at[m, x_over, 1, low], xrl.at[m, 0], x_up),
            (term.at[m, x_over, 1, high], xrl.at[m, 1], x_down),
            (xsum.at[m, 0], xf.at[m, 0, low], x_up),
            (xsum.at[m, 1], xf.at[m, 1, high], x_down),
        ][i]
        return remote(src, dst, xs_sem.at[m, i], xr_sem.at[m, i], where)

    def y_place(m):
        return lax.rem(m - y + 4, 4)

    def add_cores(m):
        crossing(m).wait()
        for goal in range(4):
            for part in range(2):
                at = slice(goal * 192 + part * 96, goal * 192 + part * 96 + 96)
                term[m, goal, part] = (
                    mine[m, at].astype(F32) + core_r[m, at].astype(F32)
                ).astype(BF16)

        @pl.when(y_place(m) == 2)
        def _():
            y_copy(m, 2).start()
            y_copy(m, 3).start()

        for i in (2, 3):
            x_copy(m, i).start()

    def send_next(m):
        @pl.when(y_place(m) == 1)
        def _():
            y_copy(m, 0).start()

        @pl.when(y_place(m) == 3)
        def _():
            y_copy(m, 1).start()

        for i in (0, 1):
            x_copy(m, i).start()

    def hand_on(m):
        @pl.when(y_place(m) == 1)
        def _():
            y_copy(m, 2).wait_recv()
            for goal in range(2):
                ysum[0, goal] = (
                    term[m, goal, 0].astype(F32) + yrl[0, goal].astype(F32)
                ).astype(BF16)
            y_copy(m, 4).start()

        @pl.when(y_place(m) == 3)
        def _():
            y_copy(m, 3).wait_recv()
            for goal in range(2):
                ysum[1, goal] = (
                    term[m, 2 + goal, 0].astype(F32) + yrl[1, goal].astype(F32)
                ).astype(BF16)
            y_copy(m, 5).start()

        for n, goal in ((0, x_next), (1, x_last)):
            x_copy(m, 2 + n).wait_recv()
            at = slice(48 * n, 48 * n + 48)
            xsum[m, n] = (
                term[m, goal, 1, at].astype(F32) + xrl[m, n].astype(F32)
            ).astype(BF16)
            x_copy(m, 4 + n).start()

    steps = {
        "C": corner_terms, "E": lambda: terms_of(2, ends), "G": send_ends, "S": side_terms,
        "K": lambda: terms_of(0, acc),
    }
    for m in range(4):
        steps["A%d" % m] = partial(add_cores, m)
        steps["B%d" % m] = partial(send_next, m)
        steps["H%d" % m] = partial(hand_on, m)
    def cross():
        for m in range(4):
            crossing(m).start()

    steps["X"] = cross
    def to_column_second(k):
        goal = lax.rem(x + k, 4)
        return remote(ta.at[goal], xa_r.at[3 - k], xas_sem.at[k - 1], xar_sem.at[3 - k],
                      device(y, goal, z, core))

    def to_row_second(m):
        slot = lax.rem(7 - y_place(m), 4)
        return remote(tb.at[m], yb_r.at[slot], ybs_sem.at[m], ybr_sem.at[slot],
                      device(m, x, z, core))

    def second_of_rows():
        for i in (0, 1, 4, 5):
            y_copy(0, i).wait_recv()
        for goal in range(4):
            total = term[y, goal, 0].astype(F32)
            ta[goal] = (total + yf[0, goal].astype(F32) + yf[1, goal].astype(F32)).astype(BF16)
        for k in (2, 1, 3):
            to_column_second(k).start()

    def second_of_columns(m):
        for i in (0, 1, 4, 5):
            x_copy(m, i).wait_recv()
        total = term[m, x, 1].astype(F32)
        tb[m] = (total + xf[m, 0].astype(F32) + xf[m, 1].astype(F32)).astype(BF16)

        @pl.when(y != m)
        def _():
            to_row_second(m).start()

    def cut(total, base):
        for i in range(4):
            for c in range(2):
                row = i * 24 + c * 12
                block = jnp.concatenate([total[row : row + 12], jnp.zeros((4, HALF), F32)], axis=0)
                zs[base + i, c] = block.astype(BF16)

    def along(k, c):
        goal = lax.rem(z + k, 8)
        return remote(zs.at[goal, c], zr.at[core, 7 - k], zs_sem.at[k, c], zr_sem.at[core, 7 - k],
                      device(y, x, goal, c))

    def across():
        return remote(zs.at[z, 1 - core], zr.at[core, 7], zs_sem.at[0, 0], zr_sem.at[core, 7],
                      sibling)

    def third():
        for k in (1, 2, 3):
            to_column_second(k).wait_recv()
        total = ta[x].astype(F32)
        for slot in range(3):
            total = total + xa_r[slot].astype(F32)
        cut(total, 0)
        for slot in range(3):
            remote(tb.at[0], yb_r.at[slot], ybs_sem.at[0], ybr_sem.at[slot], sibling).wait_recv()
        total = tb[y].astype(F32)
        for slot in range(3):
            total = total + yb_r[slot].astype(F32)
        cut(total, 4)
        for k in (4, 3, 5, 2, 6, 1, 7):
            for c in (0, 1):
                along(k, c).start()
        across().start()

    steps["Y"], steps["Z"] = second_of_rows, third
    for m in range(4):
        steps["L%d" % m] = partial(second_of_columns, m)

    loaded = set()
    for step in ORDER:
        for i in need.get(step, ()):
            if i not in loaded:
                loaded.add(i)
                loads[i].wait()
        steps[step]()

    for ry in (-1, 1):
        @pl.when(exists(0, -ry))
        def _(ry=ry):
            from_side(ry).wait_recv()
            p, c = (1, 0) if ry == 1 else (0, 1)
            for r in range(2):
                acc[2 * r + c] += side_r[p, r].astype(F32)
    for rx in (-1, 1):
        n, r = (1, 0) if rx == 1 else (0, 1)

        @pl.when(exists(-rx, 0))
        def _(rx=rx, n=n, r=r):
            for c in range(2):
                from_end(rx, c).wait_recv()
                acc[2 * r + c] += end_r[n, c].astype(F32)
    for rx, ry in ((-1, 1), (1, -1)):
        n, r = (1, 0) if rx == 1 else (0, 1)
        p, c = (1, 0) if ry == 1 else (0, 1)

        @pl.when(exists(-rx, -ry) & straight(-rx, -ry, gy))
        def _(rx=rx, ry=ry, n=n, p=p, r=r, c=c):
            remote(corner.at[0], corner_r.at[n], pass_send.at[0, 0], pass_recv.at[n, 1 - p],
                   sibling).wait_recv()
            acc[2 * r + c] += corner_r[n].astype(F32)

    ag_s[...] = acc[...].astype(BF16)
    ag_copy = pltpu.make_async_copy(ag_s, ag_out, store_sem.at[0])
    ag_copy.start()

    def arrived(c, slot):
        remote(zs.at[0, 0], zr.at[c, slot], zs_sem.at[0, 0], zr_sem.at[c, slot],
               sibling).wait_recv()
        return zr[c, slot].astype(F32)

    held = zs[z, core].astype(F32)
    for slot in range(7):
        held = held + arrived(core, slot)
    other = arrived(1 - core, 7)
    for slot in range(7):
        other = other + arrived(1 - core, slot)
    low = core == 0
    held, other = held[0:12], other[0:12]
    norm = (extents[0] * extents[1] * Q_DEV) ** (-0.5)
    wg_s[:, 0:HALF] = jnp.where(low, held, other) * norm
    wg_s[:, HALF:D] = jnp.where(low, other, held) * norm
    wg_copy = pltpu.make_async_copy(wg_s, wg_out, store_sem.at[1])
    wg_copy.start()

    for rx in (-1, 1):
        @pl.when(exists(rx, 0))
        def _(rx=rx):
            from_end(rx, 0).wait_send()
            from_end(rx, 1).wait_send()
        for ry in (-1, 1):
            @pl.when(exists(rx, ry))
            def _(rx=rx, ry=ry):
                from_corner(rx, ry, False).wait_send()
    for ry in (-1, 1):
        @pl.when(exists(0, ry))
        def _(ry=ry):
            from_side(ry).wait_send()
    for i in range(6):
        y_copy(0, i).wait_send()
    for m in range(4):
        for i in range(6):
            x_copy(m, i).wait_send()
    for k in (1, 2, 3):
        to_column_second(k).wait_send()
    for m in range(4):
        @pl.when(y != m)
        def _(m=m):
            to_row_second(m).wait_send()
    for k in range(1, 8):
        for c in (0, 1):
            along(k, c).wait_send()
    across().wait_send()
    ag_copy.wait()
    wg_copy.wait()


def grads(extents, pk, pv, w, wo, wk, wv):
    any_spec = pl.BlockSpec(memory_space=pl.ANY)
    blocks = (PAIRS, 16, TILE, TILE)
    square = (D, D)
    four, two = (4, TILE, D), (2, 2, TILE, D)
    dma = pltpu.SemaphoreType.DMA
    held = [
        (blocks, BF16), (blocks, BF16), (square, BF16), (square, BF16),
        (four, BF16), (two, BF16), (four, F32), (four, BF16), (two, BF16), (four, BF16),
        (two, BF16), ((2, TILE, D), BF16), (four, F32), (four, BF16),
        ((12, D), F32),
        ((4, D, HALF), BF16), ((4, D, HALF), BF16),
        ((4, 4, 2, 96, HALF), BF16),
        ((2, 4, 96, HALF), BF16), ((2, 2, 96, HALF), BF16), ((2, 2, 96, HALF), BF16),
        ((4, 2, 96, HALF), BF16), ((4, 2, 48, HALF), BF16), ((4, 2, 48, HALF), BF16),
        ((4, 96, HALF), BF16), ((4, 96, HALF), BF16), ((3, 96, HALF), BF16),
        ((3, 96, HALF), BF16), ((8, 2, 16, HALF), BF16), ((2, 8, 16, HALF), BF16),
    ]
    sems = [(14,), (2,), (2, 2), (2, 2), (2, 2), (2, 2), (2,), (2,), (4,), (4,), (6,), (6,),
            (4, 6), (4, 6), (3,), (3,), (4,), (3,), (8, 2), (2, 8)]
    anchor_grad, weight_grads = pl.pallas_call(
        partial(grads_kernel, extents),
        name="grads",
        out_shape=[
            jax.ShapeDtypeStruct(four, BF16),
            jax.ShapeDtypeStruct((12, D), F32),
        ],
        in_specs=[any_spec] * 6,
        out_specs=[any_spec] * 2,
        scratch_shapes=[pltpu.VMEM(s, t) for s, t in held] + [dma(s) for s in sems],
        compiler_params=pltpu.CompilerParams(
            collective_id=1, has_side_effects=True, vmem_limit_bytes=VMEM_BYTES
        ),
    )(pk, pv, w, wo, wk, wv)
    return anchor_grad, weight_grads


def settle_kernel(ag_in, wg_in, ag_out, wg_out, ag, wg, sem):
    loads = [
        pltpu.make_async_copy(ag_in.at[n], ag.at[n], sem.at[0, n]) for n in range(4)
    ] + [pltpu.make_async_copy(wg_in, wg, sem.at[0, 4])]
    stores = [
        pltpu.make_async_copy(ag.at[n], ag_out.at[n], sem.at[1, n]) for n in range(4)
    ] + [pltpu.make_async_copy(wg, wg_out, sem.at[1, 4])]
    for load in loads:
        load.start()
    for load, store in zip(loads, stores):
        load.wait()
        store.start()
    for store in stores:
        store.wait()


def settle(anchor_grad, weight_grads):
    any_spec = pl.BlockSpec(memory_space=pl.ANY)
    held = (anchor_grad, weight_grads)
    return pl.pallas_call(
        settle_kernel,
        name="settle",
        out_shape=[jax.ShapeDtypeStruct(h.shape, h.dtype) for h in held],
        in_specs=[any_spec] * 2,
        out_specs=[any_spec] * 2,
        scratch_shapes=[pltpu.VMEM(h.shape, h.dtype) for h in held]
        + [pltpu.SemaphoreType.DMA((2, 5))],
        compiler_params=pltpu.CompilerParams(vmem_limit_bytes=VMEM_BYTES),
    )(*held)


def on_device(
    extents,
    query_feats, anchors, tile_lists, tile_counts, out_grad, w_query, w_key, w_value, w_out,
):
    qf = query_feats.reshape(Q_DEV, D)
    do = out_grad.reshape(Q_DEV, D)
    order = jnp.array([HELD.index((w // 4, w % 4)) for w in range(16)], jnp.int32)
    kw, vw, awt, q, dp, dpt, qft = halo(extents, anchors, qf, do, w_query, w_key, w_value, w_out)
    pk, pv, w, wo, query_grad = attention(
        tile_lists, tile_counts, order, kw, vw, q, dp, dpt, awt, qft, do, w_query
    )
    anchor_grad, weight_grads = settle(*grads(extents, pk, pv, w, wo, w_key, w_value))
    return query_grad.reshape(query_feats.shape), anchor_grad.reshape(anchors.shape), weight_grads


def solution(mesh):
    four = P("gx", "gy", None, None)
    in_specs = (four, four, four, P("gx", "gy", None), four, P(), P(), P(), P())
    out_specs = (four, four, P(("gx", "gy"), None))
    extents = (mesh.shape["gx"], mesh.shape["gy"])
    return jax.shard_map(
        partial(on_device, extents),
        mesh=mesh, in_specs=in_specs, out_specs=out_specs, check_vma=False,
    )
```

```python
from functools import partial

import jax
import jax.numpy as jnp
from jax import lax
from jax.experimental import pallas as pl
from jax.experimental.pallas import tpu as pltpu
from jax.sharding import PartitionSpec as P

HEADS = 12
HEAD_DIM = 64
KT = 4
D = 768
TILE = 128
PAIRS = 6
Q_DEV = 512
SCALE = HEAD_DIM ** (-0.5)
HALF = 384
LOG2E = 1.4426950408889634
DEAD = 1e30
ORDER = (
    "X", "C", "A0", "B0", "A1", "B1", "S", "A2", "B2", "A3", "B3", "E", "G", "H0", "H1", "H2", "H3",
    "Y", "L0", "L1", "L2", "L3", "K", "Z",
)
MESH = pl.DeviceIdType.MESH
F32 = jnp.float32
BF16 = jnp.bfloat16
PIECES = ("q", "0", "1", "2", "o", "")
VMEM_BYTES = 56 * 1024 * 1024

DIRS = ((-1, 0), (1, 0), (-1, -1), (-1, 1), (1, -1), (1, 1), (0, -1), (0, 1))
CENTRE = ((1, 1), (1, 2), (2, 1), (2, 2))
BESIDE = ((1, 0), (2, 0), (1, 3), (2, 3))
ENDS = ((0, 1), (0, 2), (3, 1), (3, 2))
CORNERS = ((0, 0), (3, 0), (0, 3), (3, 3))
HELD = CENTRE + BESIDE + ENDS + CORNERS


def nn(left, right):
    return lax.dot_general(left, right, (((1,), (0,)), ((), ())), preferred_element_type=F32)


def nt(left, right):
    return lax.dot_general(left, right, (((1,), (1,)), ((), ())), preferred_element_type=F32)


def tn(left, right):
    return lax.dot_general(left, right, (((0,), (0,)), ((), ())), preferred_element_type=F32)


def inside(place, extents):
    (px, py), (nx, ny) = place, extents
    return (px >= 0) & (px < nx) & (py >= 0) & (py < ny)


def greet(partners, meanwhile):
    barrier = pltpu.get_barrier_semaphore()
    total = jnp.int32(0)
    for where, present in partners:
        if present is True:
            pl.semaphore_signal(barrier, inc=1, device_id=where, device_id_type=MESH)
            total = total + 1
            continue

        @pl.when(present)
        def _(where=where):
            pl.semaphore_signal(barrier, inc=1, device_id=where, device_id_type=MESH)
        total = total + jnp.where(present, 1, 0).astype(jnp.int32)
    for copy in meanwhile:
        copy.start()
    pl.semaphore_wait(barrier, total)


def straight(dx, dy, gy):
    return ((dx, dy) == (1, -1)) & (gy == 2) | ((dx, dy) == (-1, 1)) & (gy == 1)


def halo_kernel(
    extents,
    anchors, qf_in, do_in, wq_in, wk_in, wv_in, wo_in,
    kw_out, vw_out, awt_out, q_out, dp_out, dpt_out, qft_out,
    win, kw, vw, awt, qf, do, wq, wk, wv, wo, q_s, dp_s, dpt_s, qft_s,
    end_send, end_recv, side_send, side_recv, corner_send, corner_recv, load_sem, store_sem,
):
    gx, gy = lax.axis_index("gx"), lax.axis_index("gy")
    loads = [
        pltpu.make_async_copy(src, dst, load_sem.at[i])
        for i, (src, dst) in enumerate(
            [(qf_in, qf), (wq_in, wq), (do_in, do), (wo_in, wo), (wk_in, wk), (wv_in, wv)]
        )
    ]
    own = pltpu.make_async_copy(anchors, win.at[1:3, 1:3], load_sem.at[6])
    greet(
        [((gx + dx, gy + dy), inside((gx + dx, gy + dy), extents)) for dx, dy in DIRS],
        loads + [own],
    )

    def exists(dx, dy):
        return inside((gx + dx, gy + dy), extents)

    def remote(src, dst, send, recv, dx, dy):
        return pltpu.make_async_remote_copy(
            src_ref=src, dst_ref=dst, send_sem=send, recv_sem=recv,
            device_id=(gx + dx, gy + dy), device_id_type=MESH,
        )

    def to_end(dx, c):
        n, row, goal = (0, 1, 0) if dx == 1 else (1, 0, 3)
        return remote(anchors.at[row, c], win.at[goal, c + 1], end_send.at[n, c],
                      end_recv.at[n, c], dx, 0)

    def to_side(dy):
        n, col, goal = (0, 1, 0) if dy == 1 else (1, 0, 3)
        return remote(anchors.at[:, col], win.at[1:3, goal], side_send.at[n], side_recv.at[n],
                      0, dy)

    def to_corner(dx, dy, direct):
        row, goal_row = (1, 0) if dx == 1 else (0, 3)
        col, goal_col = (1, 0) if dy == 1 else (0, 3)
        n, p = int(dx == -1), int(dy == -1)
        src = anchors.at[row, col] if direct else win.at[goal_row, col + 1]
        return remote(src, win.at[goal_row, goal_col], corner_send.at[n, p],
                      corner_recv.at[n, p], dx if direct else 0, dy)

    first = jnp.where(gy < 2, 1, 0)
    for turn in range(2):
        for dx in (1, -1):
            @pl.when(exists(dx, 0))
            def _(turn=turn, dx=dx):
                to_end(dx, first if turn == 0 else 1 - first).start()
    for dx, dy in ((1, -1), (-1, 1)):
        @pl.when(exists(dx, dy) & straight(dx, dy, gy))
        def _(dx=dx, dy=dy):
            to_corner(dx, dy, True).start()
    for dy in (1, -1):
        @pl.when(exists(0, dy))
        def _(dy=dy):
            to_side(dy).start()

    for dx, dy in DIRS:
        p0, p1 = {-1: (3, 4), 0: (1, 3), 1: (0, 1)}[dx]
        q0, q1 = {-1: (3, 4), 0: (1, 3), 1: (0, 1)}[dy]

        @pl.when(jnp.logical_not(exists(-dx, -dy)))
        def _(p0=p0, p1=p1, q0=q0, q1=q1):
            win[p0:p1, q0:q1] = jnp.zeros((p1 - p0, q1 - q0, TILE, D), BF16)

    loads[0].wait()
    loads[1].wait()

    def project_query(j, _):
        at = pl.ds(pl.multiple_of(j * 256, 256), 256)
        q_s[:, at] = (nn(qf[...], wq[:, at]).astype(BF16) * SCALE).astype(BF16)
        return 0

    lax.fori_loop(0, 3, project_query, 0)
    loads[2].wait()
    loads[3].wait()

    def project_dout(j, _):
        at = pl.ds(pl.multiple_of(j * 256, 256), 256)
        dp_s[:, at] = nt(do[...], wo[at, :]).astype(BF16)
        dpt_s[at, :] = nt(wo[at, :], do[...]).astype(BF16)
        qft_s[at, :] = qf[:, at].T
        return 0

    lax.fori_loop(0, 3, project_dout, 0)
    stores = []

    def store(src, dst):
        copy = pltpu.make_async_copy(src, dst, store_sem.at[len(stores)])
        copy.start()
        stores.append(copy)

    store(q_s, q_out)
    store(dp_s, dp_out)
    store(dpt_s, dpt_out)
    store(qft_s, qft_out)
    loads[4].wait()
    loads[5].wait()
    own.wait()

    def project_tiles(places, base):
        rows = jnp.concatenate([win[r, c] for r, c in places], axis=0)
        count = len(places)

        def step(j, _):
            at = pl.ds(pl.multiple_of(j * 256, 256), 256)
            for weight, goal in ((wk, kw), (wv, vw)):
                part = nn(rows, weight[:, at]).astype(BF16)
                for n in range(count):
                    for i in range(2):
                        goal[2 * j + i, base + n] = part[
                            n * TILE : (n + 1) * TILE, i * TILE : (i + 1) * TILE
                        ]
            return 0

        lax.fori_loop(0, 3, step, 0, unroll=True)
        for n, (r, c) in enumerate(places):
            awt[:, pl.ds(pl.multiple_of((base + n) * TILE, TILE), TILE)] = win[r, c].T
        at = pl.ds(base, count)
        wide = pl.ds(pl.multiple_of(base * TILE, TILE), count * TILE)
        store(kw.at[:, at], kw_out.at[:, at])
        store(vw.at[:, at], vw_out.at[:, at])
        store(awt.at[:, wide], awt_out.at[:, wide])

    project_tiles(CENTRE, 0)
    for dy in (1, -1):
        @pl.when(exists(0, -dy))
        def _(dy=dy):
            to_side(dy).wait_recv()
    project_tiles(BESIDE, 4)
    for turn in range(2):
        for dx in (1, -1):
            c = first if turn == 0 else 1 - first

            @pl.when(exists(-dx, 0))
            def _(dx=dx, c=c):
                to_end(dx, c).wait_recv()

            for dy, col in ((1, 1), (-1, 0)):
                @pl.when(exists(-dx, 0) & exists(0, dy) & (c == col)
                         & jnp.logical_not(straight(dx, dy, gy)))
                def _(dx=dx, dy=dy):
                    to_corner(dx, dy, False).start()
    project_tiles(ENDS, 8)
    for turn in range(2):
        side = lax.rem(gy + 1 + turn, 2)
        for dy, p in ((1, 0), (-1, 1)):
            for dx in (1, -1):
                @pl.when(exists(-dx, -dy) & (side == p))
                def _(dx=dx, dy=dy):
                    to_corner(dx, dy, True).wait_recv()
        project_tiles([(0, 3 * side), (3, 3 * side)], 12 + 2 * side)
    for dx in (1, -1):
        @pl.when(exists(dx, 0))
        def _(dx=dx):
            to_end(dx, 0).wait_send()
            to_end(dx, 1).wait_send()
        for dy in (1, -1):
            here = straight(dx, dy, gy)

            @pl.when(exists(dx, dy) & here | exists(-dx, dy) & jnp.logical_not(here))
            def _(dx=dx, dy=dy):
                to_corner(dx, dy, True).wait_send()
    for dy in (1, -1):
        @pl.when(exists(0, dy))
        def _(dy=dy):
            to_side(dy).wait_send()
    for copy in stores:
        copy.wait()


def halo(extents, anchors, qf, do, wq, wk, wv, wo):
    any_spec = pl.BlockSpec(memory_space=pl.ANY)
    blocks = (PAIRS, 16, TILE, TILE)
    tall, wide = (Q_DEV, D), (D, Q_DEV)
    square = (D, D)
    shapes = [blocks, blocks, (D, 16 * TILE), tall, tall, wide, wide]
    return pl.pallas_call(
        partial(halo_kernel, extents),
        name="halo",
        out_shape=[jax.ShapeDtypeStruct(s, BF16) for s in shapes],
        in_specs=[any_spec] * 7,
        out_specs=[any_spec] * 7,
        scratch_shapes=[
            pltpu.VMEM(s, BF16)
            for s in [(4, 4, TILE, D), blocks, blocks, (D, 16 * TILE), tall, tall,
                      square, square, square, square, tall, tall, wide, wide]
        ]
        + [
            pltpu.SemaphoreType.DMA(s)
            for s in [(2, 2), (2, 2), (2,), (2,), (2, 2), (2, 2), (7,), (19,)]
        ],
        compiler_params=pltpu.CompilerParams(
            collective_id=0, has_side_effects=True, vmem_limit_bytes=VMEM_BYTES
        ),
    )(anchors, qf, do, wq, wk, wv, wo)


def attention_kernel(
    lists, counts, order, kw, vw, q_ref, dp_ref, dpt_ref, awt_in, qft_in, do_in, wq_in,
    pk_out, pv_out, w_out, wo_out, qg_out,
    dk, dv, kv, att_s, dq_s, awt, qft, do_s, wq, sem,
):
    pair = pl.program_id(0)
    loads = [
        pltpu.make_async_copy(src, dst, sem.at[i])
        for i, (src, dst) in enumerate([(qft_in, qft), (do_in, do_s), (awt_in, awt), (wq_in, wq)])
    ]

    @pl.when(pair == 0)
    def _():
        for load in loads:
            load.start()

    slot, last = lax.rem(pair, 2), lax.rem(pair + 1, 2)

    def kept(which):
        return pl.ds(pl.multiple_of(which * TILE, TILE), TILE)

    before = kept(jnp.maximum(pair - 1, 0))

    def pair_weights(i):
        at = slice(i * 256, (i + 1) * 256)
        both = nn(awt[at, :], kv[last]).astype(BF16)
        w_out[0, 1, at, :] = both[:, :TILE]
        w_out[0, 2, at, :] = both[:, TILE:]

    def query_weights():
        w_out[0, 0] = nn(qft[...], dq_s[:, before]).astype(BF16)

    def out_weights():
        wo_out[...] = nn(att_s[last], do_s[...]).astype(BF16)

    first = lax.broadcasted_iota(jnp.int32, (TILE, TILE), 1) < HEAD_DIM

    def products(b):
        tiles = [order[lists[0, 0, b, s]] for s in range(KT)]
        at = slice(b * TILE, (b + 1) * TILE)
        q, do = q_ref[at, :], dp_ref[at, :]
        zero = jnp.zeros_like(q)
        q2 = jnp.concatenate([jnp.where(first, q, zero), jnp.where(first, zero, q)], axis=0)
        do2 = jnp.concatenate([jnp.where(first, do, zero), jnp.where(first, zero, do)], axis=0)
        keys = jnp.concatenate([kw[0, t] for t in tiles], axis=0)
        values = jnp.concatenate([vw[0, t] for t in tiles], axis=0)
        return b, at, tiles, q2, do2, keys, values, nt(keys, q2), nt(values, do2)

    def softmax(state):
        b, at, tiles, q2, do2, keys, values, scores, dprob = state
        live = [s < counts[0, 0, b] for s in range(KT)]
        slots = [scores[s * TILE : (s + 1) * TILE] for s in range(KT)]
        top = jnp.max(slots[0], axis=0, keepdims=True)
        for s in range(1, KT):
            best = jnp.max(slots[s], axis=0, keepdims=True)
            top = jnp.maximum(top, jnp.where(live[s], best, -jnp.inf))
        top = top * LOG2E
        expo = jnp.concatenate(
            [
                jnp.exp2(slots[s] * LOG2E - (top + jnp.where(live[s], 0.0, DEAD).astype(F32)))
                for s in range(KT)
            ],
            axis=0,
        )
        prob = expo * (1.0 / jnp.sum(expo, axis=0, keepdims=True))
        half = prob.astype(BF16)
        att2 = tn(values, half)
        att = jnp.concatenate(
            [att2[:HEAD_DIM, :TILE], att2[HEAD_DIM:, TILE:]], axis=0
        ).astype(BF16)
        att_s[slot, :, at] = att
        both = att.astype(F32) * dpt_ref[:, at].astype(F32)
        delta = jnp.concatenate(
            [
                jnp.sum(both[:HEAD_DIM], axis=0, keepdims=True),
                jnp.sum(both[HEAD_DIM:], axis=0, keepdims=True),
            ],
            axis=1,
        )
        return at, tiles, q2, do2, keys, half, (prob * (dprob - delta)).astype(BF16)

    def gradients(state):
        at, tiles, q2, do2, keys, half, dscore = state
        dq2 = tn(keys, dscore)
        dq = jnp.concatenate([dq2[:HEAD_DIM, :TILE], dq2[HEAD_DIM:, TILE:]], axis=0) * SCALE
        dq_s[at, kept(pair)] = dq.T.astype(BF16)
        dkey = nn(dscore, q2)
        dvalue = nn(half, do2)
        for s in range(KT):
            dk[tiles[s]] += dkey[s * TILE : (s + 1) * TILE]
            dv[tiles[s]] += dvalue[s * TILE : (s + 1) * TILE]

    def all_blocks(weights):
        dk[...] = jnp.zeros_like(dk)
        dv[...] = jnp.zeros_like(dv)
        ahead, behind = {}, {}
        for turn in range(6):
            if turn < 4:
                ahead[turn] = products(turn)
            if 1 <= turn < 5:
                behind[turn - 1] = softmax(ahead.pop(turn - 1))
            if weights:
                for piece in PIECES[turn].split():
                    if piece == "q":
                        query_weights()
                    elif piece == "o":
                        out_weights()
                    else:
                        pair_weights(int(piece))
            if turn >= 2:
                gradients(behind.pop(turn - 2))
        for t in range(16):
            key_part, value_part = dk[t].astype(BF16), dv[t].astype(BF16)
            pk_out[0, t] = key_part
            pv_out[0, t] = value_part
            kv[slot, t * TILE : (t + 1) * TILE, :TILE] = key_part
            kv[slot, t * TILE : (t + 1) * TILE, TILE:] = value_part

    @pl.when(pair == 0)
    def _():
        all_blocks(False)
        for load in loads:
            load.wait()

    @pl.when((pair > 0) & (pair < PAIRS))
    def _():
        all_blocks(True)

    @pl.when(pair == PAIRS)
    def _():
        out_weights()
        query_weights()
        for i in range(3):
            pair_weights(i)
        for i in range(3):
            at = slice(i * 256, (i + 1) * 256)
            qg_out[:, at] = nt(dq_s[...], wq[at, :]).astype(BF16)


def attention(lists, counts, order, kw, vw, q, dp, dpt, awt, qft, do, wq):
    blocks = (PAIRS, 16, TILE, TILE)
    here = lambda p: jnp.minimum(p, PAIRS - 1)
    past = lambda p: jnp.maximum(p - 1, 0)
    by_pair = pl.BlockSpec((1, 16, TILE, TILE), lambda p, *_: (here(p), 0, 0, 0))
    tall = pl.BlockSpec((Q_DEV, TILE), lambda p, *_: (0, here(p)))
    wide = pl.BlockSpec((TILE, Q_DEV), lambda p, *_: (here(p), 0))
    any_spec = pl.BlockSpec(memory_space=pl.ANY)
    vmem = pltpu.VMEM
    return pl.pallas_call(
        attention_kernel,
        name="attention",
        out_shape=[
            jax.ShapeDtypeStruct(blocks, BF16),
            jax.ShapeDtypeStruct(blocks, BF16),
            jax.ShapeDtypeStruct((2, 3, D, HALF), BF16),
            jax.ShapeDtypeStruct((D, D), BF16),
            jax.ShapeDtypeStruct((Q_DEV, D), BF16),
        ],
        grid_spec=pltpu.PrefetchScalarGridSpec(
            num_scalar_prefetch=3,
            grid=(PAIRS + 1,),
            in_specs=[by_pair, by_pair, tall, tall, wide] + [any_spec] * 4,
            out_specs=[
                by_pair,
                by_pair,
                pl.BlockSpec((1, 3, D, TILE), lambda p, *_: (past(p) // 3, 0, 0, past(p) % 3)),
                pl.BlockSpec((TILE, D), lambda p, *_: (past(p), 0)),
                pl.BlockSpec((Q_DEV, D), lambda p, *_: (0, 0)),
            ],
            scratch_shapes=[
                vmem((16, TILE, TILE), F32), vmem((16, TILE, TILE), F32),
                vmem((2, 16 * TILE, 2 * TILE), BF16), vmem((2, TILE, Q_DEV), BF16),
                vmem((Q_DEV, D), BF16), vmem((D, 16 * TILE), BF16), vmem((D, Q_DEV), BF16),
                vmem((Q_DEV, D), BF16), vmem((D, D), BF16), pltpu.SemaphoreType.DMA((4,)),
            ],
        ),
        compiler_params=pltpu.CompilerParams(vmem_limit_bytes=VMEM_BYTES),
    )(lists, counts, order, kw, vw, q, dp, dpt, awt, qft, do, wq)


def grads_kernel(
    extents,
    pk_in, pv_in, w_in, wo_in, wk_in, wv_in,
    ag_out, wg_out,
    pk, pv, wk, wv,
    corner, passed, ends, end_s, end_r, side_s, side_r, corner_r, acc, ag_s, wg_s,
    mine, core_r, term, yf, yrl, ysum, xf, xrl, xsum,
    ta, tb, xa_r, yb_r, zs, zr,
    load_sem, store_sem, pass_send, pass_recv, end_send, end_recv, side_send, side_recv,
    cs_sem, cr_sem, ys_sem, yr_sem, xs_sem, xr_sem, xas_sem, xar_sem, ybs_sem, ybr_sem,
    zs_sem, zr_sem,
):
    gx, gy = lax.axis_index("gx"), lax.axis_index("gy")
    core = lax.rem(gy, 2)
    z = lax.rem(gx, 4) * 2 + gy // 2
    x = lax.rem(gx // 4, 4)
    y = gx // 16

    def device(y, x, z, core):
        return ((y * 4 + x) * 4 + z // 2, lax.rem(z, 2) * 2 + core)

    def exists(dx, dy):
        return inside((gx + dx, gy + dy), extents)

    groups = [slice(12, 16), slice(8, 12), slice(4, 8), slice(0, 4)]
    pairs = [(wk_in, wk), (wv_in, wv)]
    for at in groups:
        pairs += [(pk_in.at[:, at], pk.at[:, at]), (pv_in.at[:, at], pv.at[:, at])]
    def terms_in(m, half):
        if m < 3:
            return w_in.at[half, m]
        return wo_in.at[:, pl.ds(pl.multiple_of(half * HALF, 128), HALF)]

    pairs += [(terms_in(m, core), mine.at[m]) for m in range(4)]
    loads = [pltpu.make_async_copy(s, d, load_sem.at[i]) for i, (s, d) in enumerate(pairs)]
    sibling = device(y, x, z, 1 - core)
    fixed = [sibling]
    fixed += [device(lax.rem(y + k, 4), x, z, core) for k in (1, 2, 3)]
    fixed += [device(y, lax.rem(x + k, 4), z, core) for k in (1, 2, 3)]
    fixed += [device(y, x, lax.rem(z + k, 8), c) for k in range(1, 8) for c in (0, 1)]
    greet([((gx + dx, gy + dy), exists(dx, dy)) for dx, dy in DIRS]
          + [(where, True) for where in fixed],
          loads[0:4] + loads[6:8] + loads[10:14] + loads[4:6] + loads[8:10])

    def remote(src, dst, send, recv, where):
        return pltpu.make_async_remote_copy(
            src_ref=src, dst_ref=dst, send_sem=send, recv_sem=recv,
            device_id=where, device_id_type=MESH,
        )

    def terms_of(group, goal):
        base = 4 * group

        def side(blocks):
            return jnp.concatenate(
                [blocks[h, base : base + 4].reshape(4 * TILE, TILE) for h in range(PAIRS)], axis=1
            )

        left_k, left_v = side(pk), side(pv)

        def step(j, _):
            at = pl.ds(pl.multiple_of(j * 256, 256), 256)
            part = nt(left_k, wk[at, :]) + nt(left_v, wv[at, :])
            for n in range(4):
                goal[n, :, at] = part[n * TILE : (n + 1) * TILE].astype(goal.dtype)
            return 0

        lax.fori_loop(0, 3, step, 0)

    def from_corner(rx, ry, direct):
        n, p = int(rx == 1), int(ry == 1)
        dst = corner_r.at[n] if direct else passed.at[n, 1 - p]
        return remote(corner.at[2 * p + n], dst, pass_send.at[n, p], pass_recv.at[n, 1 - p],
                      (gx + (rx if direct else 0), gy + ry))

    def from_end(rx, c):
        n = int(rx == 1)
        return remote(end_s.at[2 * n + c], end_r.at[n, c], end_send.at[n, c], end_recv.at[n, c],
                      (gx + rx, gy))

    def from_side(ry):
        p = int(ry == 1)
        return remote(side_s.at[2 * p : 2 * p + 2], side_r.at[p], side_send.at[p],
                      side_recv.at[p], (gx, gy + ry))

    need = {
        "C": (0, 1, 2, 3), "E": (0, 1, 4, 5), "S": (0, 1, 6, 7), "K": (0, 1, 8, 9),
        "A0": (10,), "A1": (11,), "A2": (12,), "A3": (13,),
    }

    def corner_terms():
        terms_of(3, corner)
        for rx, ry in ((-1, 1), (1, -1), (-1, -1), (1, 1)):
            direct = straight(-rx, -ry, gy + ry)

            @pl.when(exists(rx, ry) & direct)
            def _(rx=rx, ry=ry):
                from_corner(rx, ry, True).start()

            @pl.when(exists(rx, ry) & jnp.logical_not(direct))
            def _(rx=rx, ry=ry):
                from_corner(rx, ry, False).start()

    def send_ends():
        first = jnp.where(gy < 2, 0, 1)
        for turn in range(2):
            c = first if turn == 0 else 1 - first
            for rx in (-1, 1):
                n = int(rx == 1)
                waits = jnp.where(
                    c == 0,
                    exists(rx, -1) & jnp.logical_not(straight(-rx, -1, gy)),
                    exists(rx, 1) & jnp.logical_not(straight(-rx, 1, gy)),
                )

                @pl.when(exists(rx, 0) & waits)
                def _(rx=rx, n=n, c=c):
                    remote(corner.at[0], passed.at[n, c], pass_send.at[0, 0],
                           pass_recv.at[n, c], sibling).wait_recv()
                    end_s[2 * n + c] = (ends[2 * n + c] + passed[n, c].astype(F32)).astype(BF16)

                @pl.when(exists(rx, 0) & jnp.logical_not(waits))
                def _(n=n, c=c):
                    end_s[2 * n + c] = ends[2 * n + c].astype(BF16)

                @pl.when(exists(rx, 0))
                def _(rx=rx, c=c):
                    from_end(rx, c).start()

    def side_terms():
        terms_of(1, side_s)
        for ry in (-1, 1):
            @pl.when(exists(0, ry))
            def _(ry=ry):
                from_side(ry).start()

    def crossing(m):
        return remote(terms_in(m, 1 - core), core_r.at[m], cs_sem.at[m], cr_sem.at[m], sibling)

    y_up, y_down = device(lax.rem(y + 1, 4), x, z, core), device(lax.rem(y + 3, 4), x, z, core)
    x_next, x_over, x_last = lax.rem(x + 1, 4), lax.rem(x + 2, 4), lax.rem(x + 3, 4)
    x_up, x_down = device(y, x_next, z, core), device(y, x_last, z, core)

    def y_copy(m, i):
        low, high = slice(0, 2), slice(2, 4)
        src, dst, where = [
            (term.at[m, high, 0], yf.at[0, high], y_up),
            (term.at[m, low, 0], yf.at[1, low], y_down),
            (term.at[m, low, 0], yrl.at[0], y_up),
            (term.at[m, high, 0], yrl.at[1], y_down),
            (ysum.at[0], yf.at[0, low], y_up),
            (ysum.at[1], yf.at[1, high], y_down),
        ][i]
        return remote(src, dst, ys_sem.at[i], yr_sem.at[i], where)

    def x_copy(m, i):
        low, high = slice(0, 48), slice(48, 96)
        src, dst, where = [
            (term.at[m, x_next, 1, high], xf.at[m, 0, high], x_up),
            (term.at[m, x_last, 1, low], xf.at[m, 1, low], x_down),
            (term.at[m, x_over, 1, low], xrl.at[m, 0], x_up),
            (term.at[m, x_over, 1, high], xrl.at[m, 1], x_down),
            (xsum.at[m, 0], xf.at[m, 0, low], x_up),
            (xsum.at[m, 1], xf.at[m, 1, high], x_down),
        ][i]
        return remote(src, dst, xs_sem.at[m, i], xr_sem.at[m, i], where)

    def y_place(m):
        return lax.rem(m - y + 4, 4)

    def add_cores(m):
        crossing(m).wait()
        for goal in range(4):
            for part in range(2):
                at = slice(goal * 192 + part * 96, goal * 192 + part * 96 + 96)
                term[m, goal, part] = (
                    mine[m, at].astype(F32) + core_r[m, at].astype(F32)
                ).astype(BF16)

        @pl.when(y_place(m) == 2)
        def _():
            y_copy(m, 2).start()
            y_copy(m, 3).start()

        for i in (2, 3):
            x_copy(m, i).start()

    def send_next(m):
        @pl.when(y_place(m) == 1)
        def _():
            y_copy(m, 0).start()

        @pl.when(y_place(m) == 3)
        def _():
            y_copy(m, 1).start()

        for i in (0, 1):
            x_copy(m, i).start()

    def hand_on(m):
        @pl.when(y_place(m) == 1)
        def _():
            y_copy(m, 2).wait_recv()
            for goal in range(2):
                ysum[0, goal] = (
                    term[m, goal, 0].astype(F32) + yrl[0, goal].astype(F32)
                ).astype(BF16)
            y_copy(m, 4).start()

        @pl.when(y_place(m) == 3)
        def _():
            y_copy(m, 3).wait_recv()
            for goal in range(2):
                ysum[1, goal] = (
                    term[m, 2 + goal, 0].astype(F32) + yrl[1, goal].astype(F32)
                ).astype(BF16)
            y_copy(m, 5).start()

        for n, goal in ((0, x_next), (1, x_last)):
            x_copy(m, 2 + n).wait_recv()
            at = slice(48 * n, 48 * n + 48)
            xsum[m, n] = (
                term[m, goal, 1, at].astype(F32) + xrl[m, n].astype(F32)
            ).astype(BF16)
            x_copy(m, 4 + n).start()

    steps = {
        "C": corner_terms, "E": lambda: terms_of(2, ends), "G": send_ends, "S": side_terms,
        "K": lambda: terms_of(0, acc),
    }
    for m in range(4):
        steps["A%d" % m] = partial(add_cores, m)
        steps["B%d" % m] = partial(send_next, m)
        steps["H%d" % m] = partial(hand_on, m)
    def cross():
        for m in range(4):
            crossing(m).start()

    steps["X"] = cross
    def to_column_second(k):
        goal = lax.rem(x + k, 4)
        return remote(ta.at[goal], xa_r.at[3 - k], xas_sem.at[k - 1], xar_sem.at[3 - k],
                      device(y, goal, z, core))

    def to_row_second(m):
        slot = lax.rem(7 - y_place(m), 4)
        return remote(tb.at[m], yb_r.at[slot], ybs_sem.at[m], ybr_sem.at[slot],
                      device(m, x, z, core))

    def second_of_rows():
        for i in (0, 1, 4, 5):
            y_copy(0, i).wait_recv()
        for goal in range(4):
            total = term[y, goal, 0].astype(F32)
            ta[goal] = (total + yf[0, goal].astype(F32) + yf[1, goal].astype(F32)).astype(BF16)
        for k in (2, 1, 3):
            to_column_second(k).start()

    def second_of_columns(m):
        for i in (0, 1, 4, 5):
            x_copy(m, i).wait_recv()
        total = term[m, x, 1].astype(F32)
        tb[m] = (total + xf[m, 0].astype(F32) + xf[m, 1].astype(F32)).astype(BF16)

        @pl.when(y != m)
        def _():
            to_row_second(m).start()

    def cut(total, base):
        for i in range(4):
            for c in range(2):
                row = i * 24 + c * 12
                block = jnp.concatenate([total[row : row + 12], jnp.zeros((4, HALF), F32)], axis=0)
                zs[base + i, c] = block.astype(BF16)

    def along(k, c):
        goal = lax.rem(z + k, 8)
        return remote(zs.at[goal, c], zr.at[core, 7 - k], zs_sem.at[k, c], zr_sem.at[core, 7 - k],
                      device(y, x, goal, c))

    def across():
        return remote(zs.at[z, 1 - core], zr.at[core, 7], zs_sem.at[0, 0], zr_sem.at[core, 7],
                      sibling)

    def third():
        for k in (1, 2, 3):
            to_column_second(k).wait_recv()
        total = ta[x].astype(F32)
        for slot in range(3):
            total = total + xa_r[slot].astype(F32)
        cut(total, 0)
        for slot in range(3):
            remote(tb.at[0], yb_r.at[slot], ybs_sem.at[0], ybr_sem.at[slot], sibling).wait_recv()
        total = tb[y].astype(F32)
        for slot in range(3):
            total = total + yb_r[slot].astype(F32)
        cut(total, 4)
        for k in (4, 3, 5, 2, 6, 1, 7):
            for c in (0, 1):
                along(k, c).start()
        across().start()

    steps["Y"], steps["Z"] = second_of_rows, third
    for m in range(4):
        steps["L%d" % m] = partial(second_of_columns, m)

    loaded = set()
    for step in ORDER:
        for i in need.get(step, ()):
            if i not in loaded:
                loaded.add(i)
                loads[i].wait()
        steps[step]()

    for ry in (-1, 1):
        @pl.when(exists(0, -ry))
        def _(ry=ry):
            from_side(ry).wait_recv()
            p, c = (1, 0) if ry == 1 else (0, 1)
            for r in range(2):
                acc[2 * r + c] += side_r[p, r].astype(F32)
    for rx in (-1, 1):
        n, r = (1, 0) if rx == 1 else (0, 1)

        @pl.when(exists(-rx, 0))
        def _(rx=rx, n=n, r=r):
            for c in range(2):
                from_end(rx, c).wait_recv()
                acc[2 * r + c] += end_r[n, c].astype(F32)
    for rx, ry in ((-1, 1), (1, -1)):
        n, r = (1, 0) if rx == 1 else (0, 1)
        p, c = (1, 0) if ry == 1 else (0, 1)

        @pl.when(exists(-rx, -ry) & straight(-rx, -ry, gy))
        def _(rx=rx, ry=ry, n=n, p=p, r=r, c=c):
            remote(corner.at[0], corner_r.at[n], pass_send.at[0, 0], pass_recv.at[n, 1 - p],
                   sibling).wait_recv()
            acc[2 * r + c] += corner_r[n].astype(F32)

    ag_s[...] = acc[...].astype(BF16)
    ag_copy = pltpu.make_async_copy(ag_s, ag_out, store_sem.at[0])
    ag_copy.start()

    def arrived(c, slot):
        remote(zs.at[0, 0], zr.at[c, slot], zs_sem.at[0, 0], zr_sem.at[c, slot],
               sibling).wait_recv()
        return zr[c, slot].astype(F32)

    held = zs[z, core].astype(F32)
    for slot in range(7):
        held = held + arrived(core, slot)
    other = arrived(1 - core, 7)
    for slot in range(7):
        other = other + arrived(1 - core, slot)
    low = core == 0
    held, other = held[0:12], other[0:12]
    norm = (extents[0] * extents[1] * Q_DEV) ** (-0.5)
    wg_s[:, 0:HALF] = jnp.where(low, held, other) * norm
    wg_s[:, HALF:D] = jnp.where(low, other, held) * norm
    wg_copy = pltpu.make_async_copy(wg_s, wg_out, store_sem.at[1])
    wg_copy.start()

    for rx in (-1, 1):
        @pl.when(exists(rx, 0))
        def _(rx=rx):
            from_end(rx, 0).wait_send()
            from_end(rx, 1).wait_send()
        for ry in (-1, 1):
            @pl.when(exists(rx, ry))
            def _(rx=rx, ry=ry):
                from_corner(rx, ry, False).wait_send()
    for ry in (-1, 1):
        @pl.when(exists(0, ry))
        def _(ry=ry):
            from_side(ry).wait_send()
    for i in range(6):
        y_copy(0, i).wait_send()
    for m in range(4):
        for i in range(6):
            x_copy(m, i).wait_send()
    for k in (1, 2, 3):
        to_column_second(k).wait_send()
    for m in range(4):
        @pl.when(y != m)
        def _(m=m):
            to_row_second(m).wait_send()
    for k in range(1, 8):
        for c in (0, 1):
            along(k, c).wait_send()
    across().wait_send()
    ag_copy.wait()
    wg_copy.wait()


def grads(extents, pk, pv, w, wo, wk, wv):
    any_spec = pl.BlockSpec(memory_space=pl.ANY)
    blocks = (PAIRS, 16, TILE, TILE)
    square = (D, D)
    four, two = (4, TILE, D), (2, 2, TILE, D)
    dma = pltpu.SemaphoreType.DMA
    held = [
        (blocks, BF16), (blocks, BF16), (square, BF16), (square, BF16),
        (four, BF16), (two, BF16), (four, F32), (four, BF16), (two, BF16), (four, BF16),
        (two, BF16), ((2, TILE, D), BF16), (four, F32), (four, BF16),
        ((12, D), F32),
        ((4, D, HALF), BF16), ((4, D, HALF), BF16),
        ((4, 4, 2, 96, HALF), BF16),
        ((2, 4, 96, HALF), BF16), ((2, 2, 96, HALF), BF16), ((2, 2, 96, HALF), BF16),
        ((4, 2, 96, HALF), BF16), ((4, 2, 48, HALF), BF16), ((4, 2, 48, HALF), BF16),
        ((4, 96, HALF), BF16), ((4, 96, HALF), BF16), ((3, 96, HALF), BF16),
        ((3, 96, HALF), BF16), ((8, 2, 16, HALF), BF16), ((2, 8, 16, HALF), BF16),
    ]
    sems = [(14,), (2,), (2, 2), (2, 2), (2, 2), (2, 2), (2,), (2,), (4,), (4,), (6,), (6,),
            (4, 6), (4, 6), (3,), (3,), (4,), (3,), (8, 2), (2, 8)]
    anchor_grad, weight_grads = pl.pallas_call(
        partial(grads_kernel, extents),
        name="grads",
        out_shape=[
            jax.ShapeDtypeStruct(four, BF16),
            jax.ShapeDtypeStruct((12, D), F32),
        ],
        in_specs=[any_spec] * 6,
        out_specs=[any_spec] * 2,
        scratch_shapes=[pltpu.VMEM(s, t) for s, t in held] + [dma(s) for s in sems],
        compiler_params=pltpu.CompilerParams(
            collective_id=1, has_side_effects=True, vmem_limit_bytes=VMEM_BYTES
        ),
    )(pk, pv, w, wo, wk, wv)
    return anchor_grad, weight_grads


def settle_kernel(ag_in, wg_in, ag_out, wg_out, ag, wg, sem):
    loads = [
        pltpu.make_async_copy(ag_in.at[n], ag.at[n], sem.at[0, n]) for n in range(4)
    ] + [pltpu.make_async_copy(wg_in, wg, sem.at[0, 4])]
    stores = [
        pltpu.make_async_copy(ag.at[n], ag_out.at[n], sem.at[1, n]) for n in range(4)
    ] + [pltpu.make_async_copy(wg, wg_out, sem.at[1, 4])]
    for load in loads:
        load.start()
    for load, store in zip(loads, stores):
        load.wait()
        store.start()
    for store in stores:
        store.wait()


def settle(anchor_grad, weight_grads):
    any_spec = pl.BlockSpec(memory_space=pl.ANY)
    held = (anchor_grad, weight_grads)
    return pl.pallas_call(
        settle_kernel,
        name="settle",
        out_shape=[jax.ShapeDtypeStruct(h.shape, h.dtype) for h in held],
        in_specs=[any_spec] * 2,
        out_specs=[any_spec] * 2,
        scratch_shapes=[pltpu.VMEM(h.shape, h.dtype) for h in held]
        + [pltpu.SemaphoreType.DMA((2, 5))],
        compiler_params=pltpu.CompilerParams(vmem_limit_bytes=VMEM_BYTES),
    )(*held)


def on_device(
    extents,
    query_feats, anchors, tile_lists, tile_counts, out_grad, w_query, w_key, w_value, w_out,
):
    qf = query_feats.reshape(Q_DEV, D)
    do = out_grad.reshape(Q_DEV, D)
    order = jnp.array([HELD.index((w // 4, w % 4)) for w in range(16)], jnp.int32)
    kw, vw, awt, q, dp, dpt, qft = halo(extents, anchors, qf, do, w_query, w_key, w_value, w_out)
    pk, pv, w, wo, query_grad = attention(
        tile_lists, tile_counts, order, kw, vw, q, dp, dpt, awt, qft, do, w_query
    )
    anchor_grad, weight_grads = settle(*grads(extents, pk, pv, w, wo, w_key, w_value))
    return query_grad.reshape(query_feats.shape), anchor_grad.reshape(anchors.shape), weight_grads


def solution(mesh):
    four = P("gx", "gy", None, None)
    in_specs = (four, four, four, P("gx", "gy", None), four, P(), P(), P(), P())
    out_specs = (four, four, P(("gx", "gy"), None))
    extents = (mesh.shape["gx"], mesh.shape["gy"])
    return jax.shard_map(
        partial(on_device, extents),
        mesh=mesh, in_specs=in_specs, out_specs=out_specs, check_vma=False,
    )
```
